128 devices in a mesh: dom: 32 (over y, x, core), grid: 4 (over z).
Axes of the slice: x: 4, y: 4, z: 4, core: 2. Of those that a mesh axis runs over, the one named last changes fastest.
Arguments:
- charges: float32 [131072], P(('dom', 'grid')), may hold values from -4 to 4
- fractions: float32 [3, 131072], P(None, ('dom', 'grid')), may hold values from 0 to 1
- bases: int32 [3, 131072], P(None, ('dom', 'grid')), may hold values from 0 to 255, as said below
- counts: int32 [128], P(('dom', 'grid')), may hold values from 256 to 1024, as said below
Outputs:
- forces: float32 [3, 131072], P(None, ('dom', 'grid'))
The draws below stay inside these ranges and needn't reach their ends.
Inputs may be any that keep to these rules, and one draw needn't show every extreme that they name: Slot r belongs to device p = r // 1024 of dom+grid; with c = p // 16 (0 .. 7) and e = p % 16, bases[0, r] lies in c * 32 .. c * 32 + 31 and bases[1, r] in e * 16 .. e * 16 + 15. `counts`: some domain is full in every draw.
All inputs are finite; a program needn't handle non-finite values.
Results may differ from the reference program's by a relative error of at most 0.0003.
Values sent between devices are 32-bit elements; how exact they have to be, the bound alone decides.
A program may use at most 64 MiB of HBM per device.

```python
import math
import jax
import jax.numpy as jnp
from jax import lax

G = 256
ATOM_DEV = 1024
DOMY = 16
BX = 32
BY = 16
ATOMS = 131072
N_DOM = 32
N_GRID = 4


def draw_bases(key, part):
    key = jax.random.fold_in(key, 11)
    subkeys = jax.random.split(key, 3)
    row_number = jnp.arange(ATOMS, dtype=jnp.int32)
    device_number = row_number // ATOM_DEV
    block_first = device_number // DOMY
    block_second = device_number % DOMY
    base_first = block_first * BX + jax.random.randint(subkeys[0], (ATOMS,), 0, BX, dtype=jnp.int32)
    base_second = block_second * BY + jax.random.randint(subkeys[1], (ATOMS,), 0, BY, dtype=jnp.int32)
    base_third = jax.random.randint(subkeys[2], (ATOMS,), 0, G, dtype=jnp.int32)
    return jnp.stack([base_first, base_second, base_third]).astype(jnp.int32)


def draw_counts(key, part):
    key = jax.random.fold_in(key, 23)
    subkeys = jax.random.split(key, 4)
    total_domains = N_DOM * N_GRID
    light_load = jax.random.randint(subkeys[0], (total_domains,), ATOM_DEV // 4, ATOM_DEV // 2 + 1, dtype=jnp.int32)
    heavy_load = ATOM_DEV - jax.random.randint(subkeys[1], (total_domains,), 0, ATOM_DEV // 8 + 1, dtype=jnp.int32)
    membrane = jax.random.randint(subkeys[2], (total_domains,), 0, 4, dtype=jnp.int32) == 0
    chosen = jax.random.randint(subkeys[3], (), 0, total_domains, dtype=jnp.int32)
    loads = jnp.where(membrane, heavy_load, light_load)
    return jnp.where(jnp.arange(total_domains, dtype=jnp.int32) == chosen, ATOM_DEV, loads).astype(jnp.int32)


def block_scale(stream_key, dims, pieces, smallest, high):
    loudness, own = 1.0, jax.random.fold_in(stream_key, 6)
    for position, blocks in pieces:
        steps = jnp.exp(jax.random.uniform(jax.random.fold_in(own, position), (blocks,), jnp.float32, smallest / len(pieces), high / len(pieces)))
        loudness = loudness * jnp.repeat(steps, dims[position] // blocks).reshape([-1 if axis == position else 1 for axis in range(len(dims))])
    return loudness


def scatter_about(stream_key, shape, deviation, limit, shards=(), held_as=jnp.bfloat16):
    entries = deviation * jax.random.normal(stream_key, shape, jnp.float32)
    if shards:
        entries = entries * block_scale(stream_key, shape, shards, -0.22, 0.18)
    return jnp.clip(entries, -limit, limit).astype(held_as)


def setup_inputs(seed: int = 0) -> dict:
    key_list = jax.random.split(jax.random.key(seed), 5)
    return {
        "charges": scatter_about(key_list[0], (ATOMS,), 0.8, 4.0, ((0, 128),), jnp.float32),
        "fractions": jnp.clip(1.0 * jax.random.uniform(key_list[1], (3, ATOMS), jnp.float32) ** block_scale(key_list[1], (3, ATOMS), ((1, 128),), -0.2, 0.2), 0.0, 1.0),
        "bases": draw_bases(jax.random.fold_in(key_list[4], 71), 0),
        "counts": draw_counts(jax.random.fold_in(key_list[4], 71), 0),
    }


ewald_beta = 0.6
field_scale = 1.0

def spline_table(fraction):
    remainder = 1.0 - fraction
    square = fraction * fraction
    cubic_term = square * fraction
    values = jnp.stack([remainder * remainder * remainder / 6.0, (3.0 * cubic_term - 6.0 * square + 4.0) / 6.0, (-3.0 * cubic_term + 3.0 * square + 3.0 * fraction + 1.0) / 6.0, cubic_term / 6.0])
    slopes = jnp.stack([-0.5 * remainder * remainder, 0.5 * (3.0 * square - 4.0 * fraction), 0.5 * (-3.0 * square + 2.0 * fraction + 1.0), 0.5 * square])
    return (values, slopes)

def signed_wave(number, length):
    return jnp.where(number < length // 2, number, number - length).astype(jnp.float32)

def bspline_modulus(number, length):
    phase_angle = number.astype(jnp.float32) * (2.0 * math.pi / length)
    return 9.0 / (2.0 + jnp.cos(phase_angle)) ** 2

def influence(wave_first, wave_second, wave_third, length, strength):
    squared = signed_wave(wave_first, length) ** 2 + signed_wave(wave_second, length) ** 2 + signed_wave(wave_third, length) ** 2
    positive = squared > 0.0
    guarded = jnp.where(positive, squared, 1.0)
    damping = jnp.exp(-(math.pi / (ewald_beta * length)) ** 2 * squared)
    moduli = bspline_modulus(wave_first, length) * bspline_modulus(wave_second, length) * bspline_modulus(wave_third, length)
    return jnp.where(positive, strength * moduli * damping / guarded, 0.0)

def site_gradient(sampled, values_first, slopes_first, values_second, slopes_second, values_third, slopes_third):
    along_third = lax.optimization_barrier(jnp.sum(sampled * values_third[None, None], axis=2))
    slope_third = lax.optimization_barrier(jnp.sum(sampled * slopes_third[None, None], axis=2))
    grad_first = lax.optimization_barrier(jnp.sum(lax.optimization_barrier(jnp.sum(along_third * values_second[None], axis=1)) * slopes_first, axis=0))
    grad_second = lax.optimization_barrier(jnp.sum(lax.optimization_barrier(jnp.sum(along_third * slopes_second[None], axis=1)) * values_first, axis=0))
    grad_third = lax.optimization_barrier(jnp.sum(lax.optimization_barrier(jnp.sum(slope_third * values_second[None], axis=1)) * values_first, axis=0))
    return jnp.stack([grad_first, grad_second, grad_third])

def reference(charges, fractions, bases, counts):
    row_number = jnp.arange(ATOMS, dtype=jnp.int32)
    alive_rows = (row_number % ATOM_DEV < counts[row_number // ATOM_DEV]).astype(jnp.float32)
    weighted = charges * alive_rows
    values_first, slopes_first = spline_table(fractions[0])
    values_second, slopes_second = spline_table(fractions[1])
    values_third, slopes_third = spline_table(fractions[2])
    offsets = jnp.arange(4, dtype=jnp.int32)
    cell_first = (bases[0][None, None, None, :] + offsets[:, None, None, None]) % G
    cell_second = (bases[1][None, None, None, :] + offsets[None, :, None, None]) % G
    cell_third = (bases[2][None, None, None, :] + offsets[None, None, :, None]) % G
    flat_index = ((cell_first * G + cell_second) * G + cell_third).astype(jnp.int32)
    shares = weighted * values_first[:, None, None, :] * values_second[None, :, None, :] * values_third[None, None, :, :]
    charge_grid = jnp.zeros((G * G * G,), jnp.float32).at[flat_index.reshape(-1)].add(shares.reshape(-1)).reshape(G, G, G)
    numbers = jnp.arange(G, dtype=jnp.int32)
    strength = field_scale * G ** 3.5 / math.sqrt(ATOMS)
    factor = influence(numbers[:, None, None], numbers[None, :, None], numbers[None, None, :], G, strength)
    spectrum = jnp.fft.fftn(charge_grid)
    potential_grid = jnp.real(jnp.fft.ifftn(spectrum * factor)).astype(jnp.float32)
    sampled = potential_grid.reshape(-1)[flat_index]
    gradient = site_gradient(sampled, values_first, slopes_first, values_second, slopes_second, values_third, slopes_third)
    return -weighted[None, :] * gradient
```

```python
import functools
import math

import jax
import jax.numpy as jnp
import numpy as np
import ml_dtypes
from jax import lax
from jax.experimental import pallas as pl
from jax.experimental.pallas import tpu as pltpu
from jax.sharding import PartitionSpec as P

G = 256
DOMX, DOMY = 8, 16
SPANX, SPANY = 32, 16
PADX, PADY = 40, 19
N = DOMX * DOMY
ATOM_DEV = 1024
LANES = 768
TILES = LANES // 128
ROWS = 2 * TILES
REPS = 72
HALF = G
ewald_beta = 0.6
field_scale = 1.0
MESH = pl.DeviceIdType.MESH
f32, bf16 = jnp.float32, jnp.bfloat16


def halves(table):
    high = table.astype(ml_dtypes.bfloat16)
    low = (table - high.astype(np.float64)).astype(ml_dtypes.bfloat16)
    return high, low


def lane_cells():
    lane = np.arange(LANES)
    y, x = lane // PADX, lane % PADX
    valid = (x < SPANX + 3) & (y < PADY)
    return x, y, valid


def self_and_pairs(first, second):
    selfs, pairs, seen = [], [], set()
    for a in range(first):
        for b in range(second):
            if (a, b) in seen:
                continue
            mirror = ((-a) % first, (-b) % second)
            seen.update([(a, b), mirror])
            (selfs if mirror == (a, b) else pairs).append((a, b))
    return selfs, pairs


def modulus(k):
    return 9.0 / (2.0 + np.cos(2.0 * np.pi * k / G)) ** 2


def signed(k):
    return np.where(k < G // 2, k, k - G).astype(np.float64)


def tables():
    out = {}
    wave = np.arange(G // 2)
    grid = np.arange(G)
    turn = 2.0 * np.pi / G
    first = np.cos(turn * (wave[:, None] * grid[None, :] % G))
    second = np.sin(turn * (wave[:, None] * grid[None, :] % G))
    second[0] = np.cos(np.pi * grid)
    out["basis"] = np.concatenate([first, second])

    x, y, valid = lane_cells()
    selfs, pairs = self_and_pairs(DOMX, DOMY)
    reps = pairs + selfs
    weight = np.array([2.0] * len(pairs) + [1.0] * len(selfs))
    kap = np.array([a for a, b in reps])
    lam = np.array([b for a, b in reps])
    source = np.arange(N)
    c, e = source // DOMY, source % DOMY
    steps = (2 * kap[:, None] * c[None, :] + lam[:, None] * e[None, :]) % 16
    angle = 2.0 * np.pi / 16 * steps
    left = np.zeros((2, 2, REPS, 2, N))
    for j in range(2):
        left[0, j, : len(reps), j] = np.cos(angle)
        left[1, j, : len(reps), j] = np.where(steps % 8 == 0, 0.0, -np.sin(angle))
    left = left.reshape(4 * REPS, 2 * N)
    out["left"], out["left_back"] = left, left.T

    phase = turn * ((kap[:, None] * x[None, :] + lam[:, None] * y[None, :]) % G)
    twiddle = np.zeros((2, REPS, LANES))
    twiddle[0, : len(reps)] = np.cos(phase) * valid
    twiddle[1, : len(reps)] = np.sin(phase) * valid
    out["twiddle"] = twiddle

    selfs_in, pairs_in = self_and_pairs(SPANX, SPANY)
    plus = pairs_in + selfs_in[:2]
    minus = [((-a) % SPANX, (-b) % SPANY) for a, b in pairs_in] + selfs_in[2:]

    def inner(modes):
        m = np.array([a for a, b in modes])
        n = np.array([b for a, b in modes])
        return 2.0 * np.pi / 32 * ((x[:, None] * m[None, :] + 2 * y[:, None] * n[None, :]) % 32)

    right = np.concatenate(
        [
            np.cos(inner(plus)),
            np.sin(inner(pairs_in)),
            np.cos(inner(selfs_in[2:])),
        ],
        axis=1,
    )
    out["right"] = right * valid[:, None]

    rate = (np.pi / (ewald_beta * G)) ** 2
    bump = np.zeros((4, REPS, HALF))
    bump[2:] = 1.0
    for row, modes in enumerate((plus, minus)):
        kx = kap[:, None] + DOMX * np.array([a for a, b in modes])[None, :]
        ky = lam[:, None] + DOMY * np.array([b for a, b in modes])[None, :]
        square = signed(kx) ** 2 + signed(ky) ** 2
        bump[row, : len(reps)] = weight[:, None] * modulus(kx) * modulus(ky) * np.exp(-rate * square)
        bump[2 + row, : len(reps)] = square
    out["bump"] = bump

    strength = field_scale * G**3.5 / math.sqrt(N * ATOM_DEV)
    along = np.zeros((N, 128))
    for j in range(2):
        k = wave.copy()
        share = np.full(N, 2.0)
        share[0] = 1.0
        if j == 1:
            k[0] = G // 2
        square = signed(k) ** 2
        along[:, j] = strength * modulus(k) * np.exp(-rate * square) * share / float(G) ** 3
        along[:, 2 + j] = square
    out["along"] = along
    return out


def split(value):
    high = value.astype(bf16)
    return high, (value - high.astype(f32)).astype(bf16)


def dot3(a, b, dims=((1,), (0,))):
    def one(p, q):
        return lax.dot_general(p, q, (dims, ((), ())), preferred_element_type=f32)

    return one(a[0], b[0]) + (one(a[0], b[1]) + one(a[1], b[0]))


def splines(u):
    rest = 1.0 - u
    square = u * u
    cube = square * u
    values = [
        rest * rest * rest / 6.0,
        (3.0 * cube - 6.0 * square + 4.0) / 6.0,
        (-3.0 * cube + 3.0 * square + 3.0 * u + 1.0) / 6.0,
        cube / 6.0,
    ]
    slopes = [
        -0.5 * rest * rest,
        0.5 * (3.0 * square - 4.0 * u),
        0.5 * (-3.0 * square + 2.0 * u + 1.0),
        0.5 * square,
    ]
    return values, slopes


def spread(rows, first, terms, wrap=None):
    shape = (rows, first.shape[1])
    offset = lax.broadcasted_iota(jnp.int32, shape, 0) - first
    if wrap:
        offset = offset & (wrap - 1)
    masks = [offset == a for a in range(4)]
    outs = []
    for term in terms:
        total = jnp.where(masks[3], term[3], 0.0)
        for a in (2, 1, 0):
            total = jnp.where(masks[a], term[a], total)
        outs.append(total)
    return outs


def body(
    charges, fractions, bases, counts, basis, left, left_back, right, twiddle, bump, along,
    out, tw, bt, send, recv, back, home, gt, sems, own,
):
    p = lax.axis_index("dom") * 4 + lax.axis_index("grid")
    barrier = pltpu.get_barrier_semaphore()

    def peer(i):
        d = lax.rem(p + i, N)
        return d, (d // 4, lax.rem(d, 4))

    def greet(i, carry):
        pl.semaphore_signal(barrier, inc=1, device_id=peer(i)[1], device_id_type=MESH)
        return carry

    lax.fori_loop(1, N, greet, 0)

    def exchange(source, target, which):
        def go(i, carry):
            d, where = peer(i)
            pltpu.make_async_remote_copy(
                src_ref=source.at[d], dst_ref=target.at[p], send_sem=sems.at[2 * which],
                recv_sem=sems.at[2 * which + 1], device_id=where, device_id_type=MESH,
            ).start()
            return carry

        lax.fori_loop(1, N, go, 0)
        mine = pltpu.make_async_copy(source.at[p], target.at[p], own)
        mine.start()
        mine.wait()
        every = pltpu.make_async_remote_copy(
            src_ref=source.at[pl.ds(0, N - 1)], dst_ref=target.at[pl.ds(0, N - 1)],
            send_sem=sems.at[2 * which], recv_sem=sems.at[2 * which + 1],
            device_id=peer(1)[1], device_id_type=MESH,
        )
        every.wait_send()
        every.wait_recv()

    values, slopes = splines(fractions[...])
    alive = lax.broadcasted_iota(jnp.int32, (1, ATOM_DEV), 1) < counts[0]
    weighted = jnp.where(alive, charges[...], 0.0)

    def row(which, terms):
        return [t[which : which + 1] for t in terms]

    wz, sz = spread(G, bases[2:3], (row(2, values), row(2, slopes)), G)
    base = (basis[0], basis[1])
    for part, table in enumerate((wz, sz)):
        high, low = split(dot3(base, split(table)))
        tw[0, part] = high
        tw[1, part] = low

    local_x = bases[0:1] - (p // DOMY) * SPANX
    local_y = bases[1:2] - lax.rem(p, DOMY) * SPANY
    wx, sx = spread(PADX, local_x, (row(0, values), row(0, slopes)))
    wy, sy = spread(24, local_y, (row(1, values), row(1, slopes)))
    charged = wx * weighted
    for y in range(0, PADY, 2):
        pieces = [charged * wy[y : y + 1]]
        if y + 1 < PADY:
            pieces.append(charged * wy[y + 1 : y + 2])
        else:
            pieces.append(jnp.zeros((8, ATOM_DEV), f32))
        piece = jnp.concatenate(pieces, axis=0)
        high, low = split(piece)
        bt[0, pl.ds(y * PADX, piece.shape[0])] = high
        bt[1, pl.ds(y * PADX, piece.shape[0])] = low

    planes = dot3((tw[0, 0], tw[1, 0]), (bt[0], bt[1]), ((1,), (1,)))
    for j in range(2):
        for t in range(TILES):
            send[:, j * TILES + t, :] = planes[j * N : (j + 1) * N, t * 128 : (t + 1) * 128]

    pl.semaphore_wait(barrier, N - 1)
    exchange(send, recv, 0)

    def gathered(buffer):
        parts = [
            jnp.concatenate([buffer[:, j * TILES + t, :] for t in range(TILES)], axis=1)
            for j in range(2)
        ]
        return jnp.concatenate(parts, axis=0)

    first = dot3((left[0], left[1]), split(gathered(recv)))
    real, imag = first[: 2 * REPS], first[2 * REPS :]
    tc = jnp.concatenate([twiddle[0]] * 2, axis=0)
    ts = jnp.concatenate([twiddle[1]] * 2, axis=0)
    turned = jnp.concatenate([real * tc + imag * ts, imag * tc - real * ts], axis=0)
    wide = (right[0], right[1])
    modes = dot3(split(turned), wide)

    mine = along[pl.ds(p, 1), :]
    lane = lax.broadcasted_iota(jnp.int32, (REPS, HALF), 1)
    paired = lane < HALF - 2
    ones, twos, cross = [], [], []
    for j in range(2):
        scale, square = mine[:, j : j + 1], mine[:, 2 + j : 3 + j]
        both = []
        for side in range(2):
            whole = bump[2 + side] + square
            positive = whole > 0.0
            both.append(
                jnp.where(positive, bump[side] * scale / jnp.where(positive, whole, 1.0), 0.0)
            )
        total = both[0] + both[1]
        ones.append(jnp.where(paired, total, both[0]))
        twos.append(jnp.where(paired, total, both[1]))
        cross.append(jnp.where(paired, both[0] - both[1], 0.0))
    f1, f2, fd = (jnp.concatenate(parts, axis=0) for parts in (ones, twos, cross))
    rc, rs = modes[: 2 * REPS, :HALF], modes[: 2 * REPS, HALF:]
    ic, is_ = modes[2 * REPS :, :HALF], modes[2 * REPS :, HALF:]
    filtered = jnp.concatenate(
        [
            jnp.concatenate([f1 * rc + fd * is_, f2 * rs - fd * ic], axis=1),
            jnp.concatenate([f1 * ic - fd * rs, fd * rc + f2 * is_], axis=1),
        ],
        axis=0,
    )
    cells = dot3(split(filtered), wide, ((1,), (1,)))
    real, imag = cells[: 2 * REPS], cells[2 * REPS :]
    turned = jnp.concatenate([real * tc - imag * ts, imag * tc + real * ts], axis=0)
    planes = dot3((left_back[0], left_back[1]), split(turned))
    for j in range(2):
        for t in range(TILES):
            back[:, j * TILES + t, :] = planes[j * N : (j + 1) * N, t * 128 : (t + 1) * 128]
    exchange(back, home, 1)

    high, low = split(gathered(home).T)
    gt[0] = high
    gt[1] = low
    chunk = 256
    for r in range(0, ATOM_DEV, chunk):
        here = slice(r, r + chunk)
        field = dot3((gt[0], gt[1]), (tw[0, 0, :, here], tw[1, 0, :, here]))
        slope = dot3((gt[0], gt[1]), (tw[0, 1, :, here], tw[1, 1, :, here]))
        sums = [jnp.zeros((8, chunk), f32) for _ in range(3)]

        def fold(part):
            return sum(part[8 * i : 8 * i + 8] for i in range(1, PADX // 8)) + part[:8]

        for y in range(PADY):
            here_y = slice(y * PADX, (y + 1) * PADX)
            sums[0] += fold(field[here_y] * sx[:, here]) * wy[y : y + 1, here]
            sums[1] += fold(field[here_y] * wx[:, here]) * sy[y : y + 1, here]
            sums[2] += fold(slope[here_y] * wx[:, here]) * wy[y : y + 1, here]
        for a in range(3):
            total = jnp.sum(sums[a], axis=0, keepdims=True)
            out[a : a + 1, here] = -weighted[:, here] * total


def solution(mesh):
    table = tables()
    pairs = {k: np.stack(halves(table[k])) for k in ("basis", "left", "left_back", "right")}
    plain = {k: table[k].astype(np.float32) for k in ("twiddle", "bump", "along")}
    vmem = pl.BlockSpec(memory_space=pltpu.VMEM)
    smem = pl.BlockSpec(memory_space=pltpu.SMEM)
    call = pl.pallas_call(
        body,
        out_shape=jax.ShapeDtypeStruct((3, ATOM_DEV), f32),
        in_specs=[vmem, vmem, vmem, smem] + [vmem] * 7,
        out_specs=vmem,
        scratch_shapes=[
            pltpu.VMEM((2, 2, G, ATOM_DEV), bf16),
            pltpu.VMEM((2, LANES, ATOM_DEV), bf16),
            pltpu.VMEM((N, ROWS, 128), f32),
            pltpu.VMEM((N, ROWS, 128), f32),
            pltpu.VMEM((N, ROWS, 128), f32),
            pltpu.VMEM((N, ROWS, 128), f32),
            pltpu.VMEM((2, LANES, G), bf16),
            pltpu.SemaphoreType.DMA((4,)),
            pltpu.SemaphoreType.DMA,
        ],
        compiler_params=pltpu.CompilerParams(
            collective_id=1, has_side_effects=True, vmem_limit_bytes=56 << 20
        ),
    )

    def local(charges, fractions, bases, counts):
        return call(
            charges.reshape(1, ATOM_DEV), fractions, bases, counts,
            pairs["basis"], pairs["left"], pairs["left_back"], pairs["right"],
            plain["twiddle"], plain["bump"], plain["along"],
        )

    placed = (
        P(("dom", "grid")),
        P(None, ("dom", "grid")),
        P(None, ("dom", "grid")),
        P(("dom", "grid")),
    )
    return jax.shard_map(
        local, mesh=mesh, in_specs=placed, out_specs=P(None, ("dom", "grid")), check_vma=False
    )
```

```python
import functools
import math

import jax
import jax.numpy as jnp
import numpy as np
import ml_dtypes
from jax import lax
from jax.experimental import pallas as pl
from jax.experimental.pallas import tpu as pltpu
from jax.sharding import PartitionSpec as P

G = 256
DOMX, DOMY = 8, 16
SPANX, SPANY = 32, 16
PADY = 19
MAIN = PADY * SPANX
RIM = 24
N = DOMX * DOMY
ATOM_DEV = 1024
LANES = 768
HALFTILE = 640
CELLS = 704
TILES = LANES // 128
REPS = 72
HALF = G
ewald_beta = 0.6
field_scale = 1.0
MESH = pl.DeviceIdType.MESH
f32, bf16 = jnp.float32, jnp.bfloat16


def halves(table):
    high = table.astype(ml_dtypes.bfloat16)
    low = (table - high.astype(np.float64)).astype(ml_dtypes.bfloat16)
    return high, low


def lane_cells():
    lane = np.arange(LANES)
    lane = np.where(lane < CELLS, lane, lane - (CELLS - HALFTILE))
    rim = np.maximum(lane - MAIN, 0)
    x = np.where(lane < MAIN, lane % SPANX, SPANX + rim // RIM)
    y = np.where(lane < MAIN, lane // SPANX, rim % RIM)
    return x, y, (x < SPANX + 3) & (y < PADY)


def self_and_pairs(first, second):
    selfs, pairs, seen = [], [], set()
    for a in range(first):
        for b in range(second):
            if (a, b) in seen:
                continue
            mirror = ((-a) % first, (-b) % second)
            seen.update([(a, b), mirror])
            (selfs if mirror == (a, b) else pairs).append((a, b))
    return selfs, pairs


def modulus(k):
    return 9.0 / (2.0 + np.cos(2.0 * np.pi * k / G)) ** 2


def signed(k):
    return np.where(k < G // 2, k, k - G).astype(np.float64)


def tables():
    out = {}
    wave = np.arange(G // 2)
    grid = np.arange(G)
    turn = 2.0 * np.pi / G
    first = np.cos(turn * (wave[:, None] * grid[None, :] % G))
    second = np.sin(turn * (wave[:, None] * grid[None, :] % G))
    second[0] = np.cos(np.pi * grid)
    out["basis"] = np.concatenate([first, second])

    x, y, valid = lane_cells()
    selfs, pairs = self_and_pairs(DOMX, DOMY)
    reps = pairs + selfs
    weight = np.array([2.0] * len(pairs) + [1.0] * len(selfs))
    kap = np.array([a for a, b in reps])
    lam = np.array([b for a, b in reps])
    source = np.arange(N)
    c, e = source // DOMY, source % DOMY
    steps = (2 * kap[:, None] * c[None, :] + lam[:, None] * e[None, :]) % 16
    angle = 2.0 * np.pi / 16 * steps
    left = np.zeros((2, REPS, N))
    left[0, : len(reps)] = np.cos(angle)
    left[1, : len(reps)] = np.where(steps % 8 == 0, 0.0, -np.sin(angle))
    left = left.reshape(2 * REPS, N)
    out["left"], out["left_back"] = left, left.T

    phase = turn * ((kap[:, None] * x[None, :] + lam[:, None] * y[None, :]) % G)
    lane = np.arange(LANES)
    twiddle = np.zeros((2, 2, REPS, LANES))
    for j, kept in enumerate((lane < CELLS, (lane < HALFTILE) | (lane >= CELLS))):
        twiddle[j, 0, : len(reps)] = np.cos(phase) * (valid & kept)
        twiddle[j, 1, : len(reps)] = np.sin(phase) * (valid & kept)
    out["twiddle"] = twiddle

    selfs_in, pairs_in = self_and_pairs(SPANX, SPANY)
    plus = pairs_in + selfs_in[:2]
    minus = [((-a) % SPANX, (-b) % SPANY) for a, b in pairs_in] + selfs_in[2:]

    def inner(modes):
        m = np.array([a for a, b in modes])
        n = np.array([b for a, b in modes])
        return 2.0 * np.pi / 32 * ((x[:, None] * m[None, :] + 2 * y[:, None] * n[None, :]) % 32)

    right = np.concatenate(
        [
            np.cos(inner(plus)),
            np.sin(inner(pairs_in)),
            np.cos(inner(selfs_in[2:])),
        ],
        axis=1,
    )
    out["right"] = right * valid[:, None]

    rate = (np.pi / (ewald_beta * G)) ** 2
    bump = np.zeros((4, REPS, HALF))
    bump[2:] = 1.0
    for row, modes in enumerate((plus, minus)):
        kx = kap[:, None] + DOMX * np.array([a for a, b in modes])[None, :]
        ky = lam[:, None] + DOMY * np.array([b for a, b in modes])[None, :]
        square = signed(kx) ** 2 + signed(ky) ** 2
        bump[row, : len(reps)] = weight[:, None] * modulus(kx) * modulus(ky) * np.exp(-rate * square)
        bump[2 + row, : len(reps)] = square
    out["bump"] = bump

    strength = field_scale * G**3.5 / math.sqrt(N * ATOM_DEV)
    along = np.zeros((N, 128))
    for j in range(2):
        k = wave.copy()
        share = np.full(N, 2.0)
        share[0] = 1.0
        if j == 1:
            k[0] = G // 2
        square = signed(k) ** 2
        along[:, j] = strength * modulus(k) * np.exp(-rate * square) * share / float(G) ** 3
        along[:, 2 + j] = square
    out["along"] = along
    return out


def split(value):
    high = value.astype(bf16)
    return high, (value - high.astype(f32)).astype(bf16)


def dot3(a, b, dims=((1,), (0,))):
    def one(p, q):
        return lax.dot_general(p, q, (dims, ((), ())), preferred_element_type=f32)

    return one(a[0], b[0]) + (one(a[0], b[1]) + one(a[1], b[0]))


def splines(u):
    rest = 1.0 - u
    square = u * u
    cube = square * u
    values = [
        rest * rest * rest / 6.0,
        (3.0 * cube - 6.0 * square + 4.0) / 6.0,
        (-3.0 * cube + 3.0 * square + 3.0 * u + 1.0) / 6.0,
        cube / 6.0,
    ]
    slopes = [
        -0.5 * rest * rest,
        0.5 * (3.0 * square - 4.0 * u),
        0.5 * (-3.0 * square + 2.0 * u + 1.0),
        0.5 * square,
    ]
    return values, slopes


def spread(rows, first, terms, wrap=None):
    shape = (rows, first.shape[1])
    offset = lax.broadcasted_iota(jnp.int32, shape, 0) - first
    if wrap:
        offset = offset & (wrap - 1)
    masks = [offset == a for a in range(4)]
    outs = []
    for term in terms:
        total = jnp.where(masks[3], term[3], 0.0)
        for a in (2, 1, 0):
            total = jnp.where(masks[a], term[a], total)
        outs.append(total)
    return outs


def body(
    charges, fractions, bases, counts, basis_any, left_any, back_any, right_any, twiddle_any, bump_any,
    along, out, basis, left, left_back, right, twiddle, bump, tw, bt, send_a, send_b, recv_a, recv_b,
    back_a, back_b, home_a, home_b, gt, sems, loads,
):
    p = lax.axis_index("dom") * 4 + lax.axis_index("grid")
    barrier = pltpu.get_barrier_semaphore()
    loading = [
        pltpu.make_async_copy(source, target, loads.at[k])
        for k, (source, target) in enumerate(
            (
                (basis_any, basis), (left_any, left), (right_any, right), (twiddle_any, twiddle),
                (bump_any, bump), (back_any, left_back),
            )
        )
    ]
    for load in loading:
        load.start()

    def peer(i):
        d = lax.rem(p + i, N)
        return d, (d // 4, lax.rem(d, 4))

    def greet(i, carry):
        pl.semaphore_signal(barrier, inc=1, device_id=peer(i)[1], device_id_type=MESH)
        return carry

    lax.fori_loop(1, N, greet, 0, unroll=8)

    def post(source, target, which):
        def go(i, carry):
            d, where = peer(i)
            pltpu.make_async_remote_copy(
                src_ref=source.at[d], dst_ref=target.at[p], send_sem=sems.at[2 * which],
                recv_sem=sems.at[2 * which + 1], device_id=where, device_id_type=MESH,
            ).start()
            return carry

        lax.fori_loop(1, N, go, 0, unroll=8)
        target[pl.ds(p, 1)] = source[pl.ds(p, 1)]

    def every(source, target, which):
        return pltpu.make_async_remote_copy(
            src_ref=source.at[pl.ds(0, N - 1)], dst_ref=target.at[pl.ds(0, N - 1)],
            send_sem=sems.at[2 * which], recv_sem=sems.at[2 * which + 1],
            device_id=peer(1)[1], device_id_type=MESH,
        )

    values, slopes = splines(fractions[...])
    alive = lax.broadcasted_iota(jnp.int32, (1, ATOM_DEV), 1) < counts[0]
    weighted = jnp.where(alive, charges[...], 0.0)

    def row(which, terms):
        return [t[which : which + 1] for t in terms]

    (wz,) = spread(G, bases[2:3], (row(2, values),), G)
    wz = split(wz)
    loading[0].wait()
    high, low = split(dot3((basis[0], basis[1]), wz))
    tw[0, 0] = high
    tw[1, 0] = low

    local_x = bases[0:1] - (p // DOMY) * SPANX
    local_y = bases[1:2] - lax.rem(p, DOMY) * SPANY
    wx, sx = spread(40, local_x, (row(0, values), row(0, slopes)))
    wy, sy = spread(RIM, local_y, (row(1, values), row(1, slopes)))
    charged = wx * weighted
    for y in range(PADY):
        high, low = split(charged[:SPANX] * wy[y : y + 1])
        bt[0, pl.ds(y * SPANX, SPANX)] = high
        bt[1, pl.ds(y * SPANX, SPANX)] = low
    rim = [charged[SPANX + a : SPANX + a + 1] * wy for a in range(3)]
    high, low = split(jnp.concatenate(rim + [jnp.zeros((CELLS - MAIN - 3 * RIM, ATOM_DEV), f32)], axis=0))
    for k, part in enumerate((high, low)):
        bt[k, pl.ds(MAIN, CELLS - MAIN)] = part
        bt[k, pl.ds(CELLS, LANES - CELLS)] = part[HALFTILE - MAIN :]

    def to_planes(rows, columns):
        return dot3(
            (tw[0, 0, rows], tw[1, 0, rows]), (bt[0, columns], bt[1, columns]), ((1,), (1,))
        )

    def put(target, value, tiles):
        for t in range(tiles):
            target[:, t, :] = value[:, t * 128 : (t + 1) * 128]

    shared = to_planes(slice(0, G), slice(HALFTILE, LANES))
    side = lax.broadcasted_iota(jnp.int32, (N, 128), 1) < 64
    put(send_a, to_planes(slice(0, N), slice(0, HALFTILE)), TILES - 1)
    send_a[:, TILES - 1, :] = jnp.where(side, shared[:N], shared[N:])
    pl.semaphore_wait(barrier, N - 1)
    post(send_a, recv_a, 0)
    put(send_b, to_planes(slice(N, G), slice(0, HALFTILE)), TILES - 1)
    post(send_b, recv_b, 1)

    for load in loading[1:]:
        load.wait()
    mine = along[pl.ds(p, 1), :]
    lane = lax.broadcasted_iota(jnp.int32, (REPS, HALF), 1)
    paired = lane < HALF - 2
    factors = []
    for j in range(2):
        scale, square = mine[:, j : j + 1], mine[:, 2 + j : 3 + j]
        both = []
        for end in range(2):
            whole = bump[2 + end] + square
            positive = whole > 0.0
            both.append(
                jnp.where(positive, bump[end] * scale / jnp.where(positive, whole, 1.0), 0.0)
            )
        total = both[0] + both[1]
        factors.append(
            (
                jnp.where(paired, total, both[0]),
                jnp.where(paired, total, both[1]),
                jnp.where(paired, both[0] - both[1], 0.0),
            )
        )
    (sz,) = spread(G, bases[2:3], (row(2, slopes),), G)
    high, low = split(dot3((basis[0], basis[1]), split(sz)))
    tw[0, 1] = high
    tw[1, 1] = low

    def filtered(tiles, j):
        high, low = split(jnp.concatenate(tiles, axis=1))
        first = dot3((left[0], left[1]), (high, low))
        real, imag = first[:REPS], first[REPS:]
        tc, ts = twiddle[j, 0], twiddle[j, 1]
        turned = jnp.concatenate([real * tc + imag * ts, imag * tc - real * ts], axis=0)
        wide = (right[0], right[1])
        modes = dot3(split(turned), wide)
        f1, f2, fd = factors[j]
        rc, rs = modes[:REPS, :HALF], modes[:REPS, HALF:]
        ic, is_ = modes[REPS:, :HALF], modes[REPS:, HALF:]
        modes = jnp.concatenate(
            [
                jnp.concatenate([f1 * rc + fd * is_, f2 * rs - fd * ic], axis=1),
                jnp.concatenate([f1 * ic - fd * rs, fd * rc + f2 * is_], axis=1),
            ],
            axis=0,
        )
        cells = dot3(split(modes), wide, ((1,), (1,)))
        real, imag = cells[:REPS], cells[REPS:]
        turned = jnp.concatenate([real * tc - imag * ts, imag * tc + real * ts], axis=0)
        return dot3((left_back[0], left_back[1]), split(turned))

    every(send_a, recv_a, 0).wait_recv()
    plane = filtered([recv_a[:, t, :] for t in range(TILES)], 0)
    put(back_a, plane, TILES - 1)
    back_b[:, TILES - 1, :] = plane[:, HALFTILE:]
    post(back_a, home_a, 2)
    every(send_b, recv_b, 1).wait_recv()
    plane = filtered([recv_b[:, t, :] for t in range(TILES - 1)] + [recv_a[:, TILES - 1, :]], 1)
    put(back_b, plane, TILES - 1)
    back_b[:, TILES - 1, :] += plane[:, HALFTILE:]
    post(back_b, home_b, 3)

    every(send_a, recv_a, 0).wait_send()
    every(send_b, recv_b, 1).wait_send()
    every(back_a, home_a, 2).wait_recv()
    for t in range(TILES - 1):
        high, low = split(home_a[:, t, :].T)
        gt[0, pl.ds(t * 128, 128), :N] = high
        gt[1, pl.ds(t * 128, 128), :N] = low
    every(back_b, home_b, 3).wait_recv()
    for t in range(TILES - 1):
        high, low = split(home_b[:, t, :].T)
        gt[0, pl.ds(t * 128, 128), N:] = high
        gt[1, pl.ds(t * 128, 128), N:] = low
    for k, part in enumerate(split(home_b[:, TILES - 1, :].T)):
        gt[k, HALFTILE:, :N] = part[:64]
        gt[k, HALFTILE:, N:] = part[64:]
    chunk = 256
    for r in range(0, ATOM_DEV, chunk):
        here = slice(r, r + chunk)
        field = dot3((gt[0], gt[1]), (tw[0, 0, :, here], tw[1, 0, :, here]))
        slope = dot3((gt[0], gt[1]), (tw[0, 1, :, here], tw[1, 1, :, here]))
        sums = [jnp.zeros((8, chunk), f32) for _ in range(3)]

        def fold(part):
            return sum(part[8 * i : 8 * i + 8] for i in range(1, part.shape[0] // 8)) + part[:8]

        for y in range(PADY):
            cells = slice(y * SPANX, (y + 1) * SPANX)
            inner = fold(field[cells] * wx[:SPANX, here])
            sums[0] += fold(field[cells] * sx[:SPANX, here]) * wy[y : y + 1, here]
            sums[1] += inner * sy[y : y + 1, here]
            sums[2] += fold(slope[cells] * wx[:SPANX, here]) * wy[y : y + 1, here]
        for a in range(3):
            cells = slice(MAIN + a * RIM, MAIN + (a + 1) * RIM)
            x = slice(SPANX + a, SPANX + a + 1)
            sums[0] += fold(field[cells] * wy[:, here]) * sx[x, here]
            sums[1] += fold(field[cells] * sy[:, here]) * wx[x, here]
            sums[2] += fold(slope[cells] * wy[:, here]) * wx[x, here]
        for a in range(3):
            total = jnp.sum(sums[a], axis=0, keepdims=True)
            out[a : a + 1, here] = -weighted[:, here] * total
    every(back_a, home_a, 2).wait_send()
    every(back_b, home_b, 3).wait_send()


def solution(mesh):
    table = tables()
    pairs = {k: np.stack(halves(table[k])) for k in ("basis", "left", "left_back", "right")}
    plain = {k: table[k].astype(np.float32) for k in ("twiddle", "bump", "along")}
    held = [pairs[k] for k in ("basis", "left", "left_back", "right")]
    held += [plain["twiddle"], plain["bump"]]
    vmem = pl.BlockSpec(memory_space=pltpu.VMEM)
    smem = pl.BlockSpec(memory_space=pltpu.SMEM)
    anywhere = pl.BlockSpec(memory_space=pl.ANY)
    five, six = (pltpu.VMEM((N, rows, 128), f32) for rows in (TILES - 1, TILES))
    call = pl.pallas_call(
        body,
        out_shape=jax.ShapeDtypeStruct((3, ATOM_DEV), f32),
        in_specs=[vmem, vmem, vmem, smem] + [anywhere] * 6 + [vmem],
        out_specs=vmem,
        scratch_shapes=[pltpu.VMEM(a.shape, bf16 if a.dtype != np.float32 else f32) for a in held]
        + [
            pltpu.VMEM((2, 2, G, ATOM_DEV), bf16),
            pltpu.VMEM((2, LANES, ATOM_DEV), bf16),
            six, five, six, five,
            five, six, five, six,
            pltpu.VMEM((2, CELLS, G), bf16),
            pltpu.SemaphoreType.DMA((8,)),
            pltpu.SemaphoreType.DMA((6,)),
        ],
        compiler_params=pltpu.CompilerParams(
            collective_id=1, has_side_effects=True, vmem_limit_bytes=56 << 20
        ),
    )

    def local(charges, fractions, bases, counts):
        return call(
            charges.reshape(1, ATOM_DEV), fractions, bases, counts, *held, plain["along"]
        )

    placed = (
        P(("dom", "grid")),
        P(None, ("dom", "grid")),
        P(None, ("dom", "grid")),
        P(("dom", "grid")),
    )
    return jax.shard_map(
        local, mesh=mesh, in_specs=placed, out_specs=P(None, ("dom", "grid")), check_vma=False
    )
```

```python
import functools
import math

import jax
import jax.numpy as jnp
import numpy as np
import ml_dtypes
from jax import lax
from jax.experimental import pallas as pl
from jax.experimental.pallas import tpu as pltpu
from jax.sharding import PartitionSpec as P

G = 256
DOMX, DOMY = 8, 16
SPANX, SPANY = 32, 16
PADY = 19
MAIN = PADY * SPANX
RIM = 24
N = DOMX * DOMY
ATOM_DEV = 1024
LANES = 768
HALFTILE = 640
CELLS = 704
TILES = LANES // 128
REPS = 72
HALF = G
ewald_beta = 0.6
field_scale = 1.0
MESH = pl.DeviceIdType.MESH
f32, bf16 = jnp.float32, jnp.bfloat16


def halves(table):
    high = table.astype(ml_dtypes.bfloat16)
    low = (table - high.astype(np.float64)).astype(ml_dtypes.bfloat16)
    return high, low


def lane_cells():
    lane = np.arange(LANES)
    lane = np.where(lane < CELLS, lane, lane - (CELLS - HALFTILE))
    rim = np.maximum(lane - MAIN, 0)
    x = np.where(lane < MAIN, lane % SPANX, SPANX + rim // RIM)
    y = np.where(lane < MAIN, lane // SPANX, rim % RIM)
    return x, y, (x < SPANX + 3) & (y < PADY)


def self_and_pairs(first, second):
    selfs, pairs, seen = [], [], set()
    for a in range(first):
        for b in range(second):
            if (a, b) in seen:
                continue
            mirror = ((-a) % first, (-b) % second)
            seen.update([(a, b), mirror])
            (selfs if mirror == (a, b) else pairs).append((a, b))
    return selfs, pairs


def modulus(k):
    return 9.0 / (2.0 + np.cos(2.0 * np.pi * k / G)) ** 2


def signed(k):
    return np.where(k < G // 2, k, k - G).astype(np.float64)


def tables():
    out = {}
    wave = np.arange(G // 2)
    grid = np.arange(G)
    turn = 2.0 * np.pi / G
    first = np.cos(turn * (wave[:, None] * grid[None, :] % G))
    second = np.sin(turn * (wave[:, None] * grid[None, :] % G))
    second[0] = np.cos(np.pi * grid)
    out["basis"] = np.concatenate([first, second])

    x, y, valid = lane_cells()
    selfs, pairs = self_and_pairs(DOMX, DOMY)
    reps = pairs + selfs
    weight = np.array([2.0] * len(pairs) + [1.0] * len(selfs))
    kap = np.array([a for a, b in reps])
    lam = np.array([b for a, b in reps])
    source = np.arange(N)
    c, e = source // DOMY, source % DOMY
    steps = (2 * kap[:, None] * c[None, :] + lam[:, None] * e[None, :]) % 16
    angle = 2.0 * np.pi / 16 * steps
    left = np.zeros((2, REPS, N))
    left[0, : len(reps)] = np.cos(angle)
    left[1, : len(reps)] = np.where(steps % 8 == 0, 0.0, -np.sin(angle))
    left = left.reshape(2 * REPS, N)
    out["left"], out["left_back"] = left, left.T

    phase = turn * ((kap[:, None] * x[None, :] + lam[:, None] * y[None, :]) % G)
    lane = np.arange(LANES)
    twiddle = np.zeros((2, 2, REPS, LANES))
    for j, kept in enumerate((lane < CELLS, (lane < HALFTILE) | (lane >= CELLS))):
        twiddle[j, 0, : len(reps)] = np.cos(phase) * (valid & kept)
        twiddle[j, 1, : len(reps)] = np.sin(phase) * (valid & kept)
    out["twiddle"] = twiddle

    selfs_in, pairs_in = self_and_pairs(SPANX, SPANY)
    plus = pairs_in + selfs_in[:2]
    minus = [((-a) % SPANX, (-b) % SPANY) for a, b in pairs_in] + selfs_in[2:]

    def inner(modes):
        m = np.array([a for a, b in modes])
        n = np.array([b for a, b in modes])
        return 2.0 * np.pi / 32 * ((x[:, None] * m[None, :] + 2 * y[:, None] * n[None, :]) % 32)

    right = np.concatenate(
        [
            np.cos(inner(plus)),
            np.sin(inner(pairs_in)),
            np.cos(inner(selfs_in[2:])),
        ],
        axis=1,
    )
    out["right"] = right * valid[:, None]

    rate = (np.pi / (ewald_beta * G)) ** 2
    bump = np.zeros((4, REPS, HALF))
    bump[2:] = 1.0
    for row, modes in enumerate((plus, minus)):
        kx = kap[:, None] + DOMX * np.array([a for a, b in modes])[None, :]
        ky = lam[:, None] + DOMY * np.array([b for a, b in modes])[None, :]
        square = signed(kx) ** 2 + signed(ky) ** 2
        bump[row, : len(reps)] = weight[:, None] * modulus(kx) * modulus(ky) * np.exp(-rate * square)
        bump[2 + row, : len(reps)] = square
    out["bump"] = bump

    strength = field_scale * G**3.5 / math.sqrt(N * ATOM_DEV)
    along = np.zeros((N, 128))
    for j in range(2):
        k = wave.copy()
        share = np.full(N, 2.0)
        share[0] = 1.0
        if j == 1:
            k[0] = G // 2
        square = signed(k) ** 2
        along[:, j] = strength * modulus(k) * np.exp(-rate * square) * share / float(G) ** 3
        along[:, 2 + j] = square
    out["along"] = along
    return out


def far_first():
    hops = (0, 1, 2, 1)
    offsets = [(y, x, c, z) for y in range(4) for x in range(4) for c in range(2) for z in range(4)]
    spread_out = np.random.RandomState(1).permutation(len(offsets))
    offsets = [offsets[k] for k in spread_out if any(offsets[k])]
    return sorted(offsets, key=lambda o: -(hops[o[0]] + hops[o[1]] + hops[o[3]]))


def split(value):
    high = value.astype(bf16)
    return high, (value - high.astype(f32)).astype(bf16)


def dot3(a, b, dims=((1,), (0,))):
    def one(p, q):
        return lax.dot_general(p, q, (dims, ((), ())), preferred_element_type=f32)

    return one(a[0], b[0]) + (one(a[0], b[1]) + one(a[1], b[0]))


def splines(u):
    rest = 1.0 - u
    square = u * u
    cube = square * u
    values = [
        rest * rest * rest / 6.0,
        (3.0 * cube - 6.0 * square + 4.0) / 6.0,
        (-3.0 * cube + 3.0 * square + 3.0 * u + 1.0) / 6.0,
        cube / 6.0,
    ]
    slopes = [
        -0.5 * rest * rest,
        0.5 * (3.0 * square - 4.0 * u),
        0.5 * (-3.0 * square + 2.0 * u + 1.0),
        0.5 * square,
    ]
    return values, slopes


def spread(rows, first, terms, wrap=None):
    shape = (rows, first.shape[1])
    offset = lax.broadcasted_iota(jnp.int32, shape, 0) - first
    if wrap:
        offset = offset & (wrap - 1)
    masks = [offset == a for a in range(4)]
    outs = []
    for term in terms:
        total = jnp.where(masks[3], term[3], 0.0)
        for a in (2, 1, 0):
            total = jnp.where(masks[a], term[a], total)
        outs.append(total)
    return outs


def body(
    charges_any, fractions_any, bases_any, counts, basis_any, left_any, back_any, right_any, twiddle_any,
    bump_any, along_any, out, basis, left, left_back, right, twiddle, bump, along,
    charges, fractions, bases, tw, bt, send_a, send_b, recv_a, recv_b,
    back_a, back_b, home_a, home_b, gt, early, sems, loads,
):
    dom, z = lax.axis_index("dom"), lax.axis_index("grid")
    p = dom * 4 + z
    barrier = pltpu.get_barrier_semaphore()
    loading = [
        pltpu.make_async_copy(source, target, loads.at[k])
        for k, (source, target) in enumerate(
            (
                (fractions_any, fractions), (bases_any, bases), (charges_any, charges), (basis_any, basis),
                (left_any, left), (right_any, right), (twiddle_any, twiddle),
                (bump_any, bump), (along_any, along), (back_any, left_back),
            )
        )
    ]
    for load in loading:
        load.start()

    ys = [lax.rem(dom // 8 + k, 4) * 8 for k in range(4)]
    xs = [lax.rem(lax.rem(dom, 8) // 2 + k, 4) * 2 for k in range(4)]
    cores = [lax.rem(dom + k, 2) for k in range(2)]
    zs = [lax.rem(z + k, 4) for k in range(4)]
    chips = [[a + b for b in xs] for a in ys]
    peers = [(chips[a][b] + cores[c], zs[k]) for a, b, c, k in far_first()]

    for where in peers:
        pl.semaphore_signal(barrier, inc=1, device_id=where, device_id_type=MESH)

    def post(source, target, which):
        for where in peers:
            pltpu.make_async_remote_copy(
                src_ref=source.at[where[0] * 4 + where[1]], dst_ref=target.at[p],
                send_sem=sems.at[2 * which], recv_sem=sems.at[2 * which + 1],
                device_id=where, device_id_type=MESH,
            ).start()
        target[pl.ds(p, 1)] = source[pl.ds(p, 1)]

    def every(source, target, which):
        return pltpu.make_async_remote_copy(
            src_ref=source.at[pl.ds(0, N - 1)], dst_ref=target.at[pl.ds(0, N - 1)],
            send_sem=sems.at[2 * which], recv_sem=sems.at[2 * which + 1],
            device_id=peers[0], device_id_type=MESH,
        )

    for load in loading[:3]:
        load.wait()
    values, slopes = splines(fractions[...])
    alive = lax.broadcasted_iota(jnp.int32, (1, ATOM_DEV), 1) < counts[0]
    weighted = jnp.where(alive, charges[...], 0.0)

    def row(which, terms):
        return [t[which : which + 1] for t in terms]

    (wz,) = spread(G, bases[2:3], (row(2, values),), G)
    wz = split(wz)
    loading[3].wait()
    high, low = split(dot3((basis[0], basis[1]), wz))
    tw[0, 0] = high
    tw[1, 0] = low

    local_x = bases[0:1] - (p // DOMY) * SPANX
    local_y = bases[1:2] - lax.rem(p, DOMY) * SPANY
    wx, sx = spread(40, local_x, (row(0, values), row(0, slopes)))
    wy, sy = spread(RIM, local_y, (row(1, values), row(1, slopes)))
    charged = wx * weighted
    for y in range(PADY):
        high, low = split(charged[:SPANX] * wy[y : y + 1])
        bt[0, pl.ds(y * SPANX, SPANX)] = high
        bt[1, pl.ds(y * SPANX, SPANX)] = low
    rim = [charged[SPANX + a : SPANX + a + 1] * wy for a in range(3)]
    high, low = split(jnp.concatenate(rim + [jnp.zeros((CELLS - MAIN - 3 * RIM, ATOM_DEV), f32)], axis=0))
    for k, part in enumerate((high, low)):
        bt[k, pl.ds(MAIN, CELLS - MAIN)] = part

    planes = dot3((bt[0], bt[1]), (tw[0, 0], tw[1, 0]), ((1,), (1,)))

    def put(target, value, tiles):
        for t in range(tiles):
            target[:, t, :] = value[:, t * 128 : (t + 1) * 128]

    def put_turned(target, value):
        for t in range(TILES - 1):
            target[:, t, :] = value[t * 128 : (t + 1) * 128].T

    put_turned(send_a, planes[:, :N])
    send_a[:, TILES - 1, :] = jnp.concatenate([planes[HALFTILE:, :N], planes[HALFTILE:, N:]], axis=0).T
    pl.semaphore_wait(barrier, N - 1)
    post(send_a, recv_a, 0)
    put_turned(send_b, planes[:, N:])
    post(send_b, recv_b, 1)

    for load in loading[4:]:
        load.wait()
    mine = along[pl.ds(p, 1), :]
    lane = lax.broadcasted_iota(jnp.int32, (REPS, HALF), 1)
    paired = lane < HALF - 2
    factors = []
    for j in range(2):
        scale, square = mine[:, j : j + 1], mine[:, 2 + j : 3 + j]
        both = []
        for end in range(2):
            whole = bump[2 + end] + square
            positive = whole > 0.0
            both.append(
                jnp.where(positive, bump[end] * scale / jnp.where(positive, whole, 1.0), 0.0)
            )
        total = both[0] + both[1]
        factors.append(
            (
                jnp.where(paired, total, both[0]),
                jnp.where(paired, total, both[1]),
                jnp.where(paired, both[0] - both[1], 0.0),
            )
        )
    (sz,) = spread(G, bases[2:3], (row(2, slopes),), G)
    high, low = split(dot3((basis[0], basis[1]), split(sz)))
    tw[0, 1] = high
    tw[1, 1] = low

    def filtered(tiles, j):
        high, low = split(jnp.concatenate(tiles, axis=1))
        first = dot3((left[0], left[1]), (high, low))
        real, imag = first[:REPS], first[REPS:]
        tc, ts = twiddle[j, 0], twiddle[j, 1]
        turned = jnp.concatenate([real * tc + imag * ts, imag * tc - real * ts], axis=0)
        wide = (right[0], right[1])
        modes = dot3(split(turned), wide)
        f1, f2, fd = factors[j]
        rc, rs = modes[:REPS, :HALF], modes[:REPS, HALF:]
        ic, is_ = modes[REPS:, :HALF], modes[REPS:, HALF:]
        modes = jnp.concatenate(
            [
                jnp.concatenate([f1 * rc + fd * is_, f2 * rs - fd * ic], axis=1),
                jnp.concatenate([f1 * ic - fd * rs, fd * rc + f2 * is_], axis=1),
            ],
            axis=0,
        )
        cells = dot3(split(modes), wide, ((1,), (1,)))
        real, imag = cells[:REPS], cells[REPS:]
        turned = jnp.concatenate([real * tc - imag * ts, imag * tc + real * ts], axis=0)
        return dot3((left_back[0], left_back[1]), split(turned))

    every(send_a, recv_a, 0).wait_recv()
    plane = filtered([recv_a[:, t, :] for t in range(TILES)], 0)
    put(back_a, plane, TILES - 1)
    back_b[:, TILES - 1, :] = plane[:, HALFTILE:]
    post(back_a, home_a, 2)
    every(send_b, recv_b, 1).wait_recv()
    plane = filtered([recv_b[:, t, :] for t in range(TILES - 1)] + [recv_a[:, TILES - 1, :]], 1)
    put(back_b, plane, TILES - 1)
    back_b[:, TILES - 1, :] += plane[:, HALFTILE:]
    post(back_b, home_b, 3)

    every(send_a, recv_a, 0).wait_send()
    every(send_b, recv_b, 1).wait_send()
    chunk = 256

    def fold(part):
        return sum(part[8 * i : 8 * i + 8] for i in range(1, part.shape[0] // 8)) + part[:8]

    def gather(here, field, slope):
        sums = [jnp.zeros((8, chunk), f32) for _ in range(3)]
        for y in range(PADY):
            cells = slice(y * SPANX, (y + 1) * SPANX)
            inner = fold(field[cells] * wx[:SPANX, here])
            sums[0] += fold(field[cells] * sx[:SPANX, here]) * wy[y : y + 1, here]
            sums[1] += inner * sy[y : y + 1, here]
            sums[2] += fold(slope[cells] * wx[:SPANX, here]) * wy[y : y + 1, here]
        for a in range(3):
            cells = slice(MAIN + a * RIM, min(MAIN + (a + 1) * RIM, field.shape[0]))
            if cells.start >= field.shape[0]:
                continue
            x = slice(SPANX + a, SPANX + a + 1)
            rows = slice(0, cells.stop - cells.start)
            sums[0] += fold(field[cells] * wy[rows, here]) * sx[x, here]
            sums[1] += fold(field[cells] * sy[rows, here]) * wx[x, here]
            sums[2] += fold(slope[cells] * wy[rows, here]) * wx[x, here]
        return sums

    def gather_tail(sums, here, field, slope):
        for row in range(HALFTILE, MAIN + 3 * RIM, 8):
            a, y = (row - MAIN) // RIM, (row - MAIN) % RIM
            x, rows = slice(SPANX + a, SPANX + a + 1), slice(y, y + 8)
            cells = slice(row - HALFTILE, row - HALFTILE + 8)
            sums[0] += field[cells] * wy[rows, here] * sx[x, here]
            sums[1] += field[cells] * sy[rows, here] * wx[x, here]
            sums[2] += slope[cells] * wy[rows, here] * wx[x, here]

    def dot(a, b):
        return jnp.dot(a, b, preferred_element_type=f32)

    def columns(j, part, here):
        rows = slice(j * N, (j + 1) * N)
        high = tw[0, part, rows, here]
        return jnp.concatenate([high, high], axis=0), tw[1, part, rows, here]

    def fields(j, part, here):
        twice, low = columns(j, part, here)
        return dot(gt[j, :HALFTILE], twice) + dot(gt[j, :HALFTILE, :N], low)

    def turn(home, j):
        for t in range(TILES - 1):
            rows = pl.ds(t * 128, 128)
            gt[j, rows, :N], gt[j, rows, N:] = split(home[:, t, :].T)

    chunks = [slice(r, r + chunk) for r in range(0, ATOM_DEV, chunk)]
    every(back_a, home_a, 2).wait_recv()
    turn(home_a, 0)
    for here in chunks:
        for a, part in enumerate(gather(here, fields(0, 0, here), fields(0, 1, here))):
            early[a, :, here] = part
    every(back_b, home_b, 3).wait_recv()
    turn(home_b, 1)
    shared = home_b[:, TILES - 1, :].T
    shared = split(jnp.concatenate([shared[:64], shared[64:]], axis=1))
    for here in chunks:
        sums = gather(here, fields(1, 0, here), fields(1, 1, here))
        tails = [dot3(shared, (tw[0, k, :, here], tw[1, k, :, here])) for k in range(2)]
        gather_tail(sums, here, *tails)
        for a in range(3):
            total = jnp.sum(sums[a] + early[a, :, here], axis=0, keepdims=True)
            out[a : a + 1, here] = -weighted[:, here] * total
    every(back_a, home_a, 2).wait_send()
    every(back_b, home_b, 3).wait_send()


def solution(mesh):
    table = tables()
    pairs = {k: np.stack(halves(table[k])) for k in ("basis", "left", "left_back", "right")}
    plain = {k: table[k].astype(np.float32) for k in ("twiddle", "bump", "along")}
    held = [pairs[k] for k in ("basis", "left", "left_back", "right")]
    held += [plain["twiddle"], plain["bump"], plain["along"]]
    vmem = pl.BlockSpec(memory_space=pltpu.VMEM)
    smem = pl.BlockSpec(memory_space=pltpu.SMEM)
    anywhere = pl.BlockSpec(memory_space=pl.ANY)
    five, six = (pltpu.VMEM((N, rows, 128), f32) for rows in (TILES - 1, TILES))
    call = pl.pallas_call(
        body,
        out_shape=jax.ShapeDtypeStruct((3, ATOM_DEV), f32),
        in_specs=[anywhere] * 3 + [smem] + [anywhere] * 7,
        out_specs=vmem,
        scratch_shapes=[pltpu.VMEM(a.shape, bf16 if a.dtype != np.float32 else f32) for a in held]
        + [
            pltpu.VMEM((1, ATOM_DEV), f32),
            pltpu.VMEM((3, ATOM_DEV), f32),
            pltpu.VMEM((3, ATOM_DEV), jnp.int32),
            pltpu.VMEM((2, 2, G, ATOM_DEV), bf16),
            pltpu.VMEM((2, CELLS, ATOM_DEV), bf16),
            six, five, six, five,
            five, six, five, six,
            pltpu.VMEM((2, HALFTILE, G), bf16),
            pltpu.VMEM((3, 8, ATOM_DEV), f32),
            pltpu.SemaphoreType.DMA((8,)),
            pltpu.SemaphoreType.DMA((10,)),
        ],
        compiler_params=pltpu.CompilerParams(
            collective_id=1, has_side_effects=True, vmem_limit_bytes=56 << 20
        ),
    )

    def local(charges, fractions, bases, counts):
        return call(
            charges.reshape(1, ATOM_DEV), fractions, bases, counts, *held
        )

    placed = (
        P(("dom", "grid")),
        P(None, ("dom", "grid")),
        P(None, ("dom", "grid")),
        P(("dom", "grid")),
    )
    return jax.shard_map(
        local, mesh=mesh, in_specs=placed, out_specs=P(None, ("dom", "grid")), check_vma=False
    )
```

```python
import functools
import math

import jax
import jax.numpy as jnp
import numpy as np
import ml_dtypes
from jax import lax
from jax.experimental import pallas as pl
from jax.experimental.pallas import tpu as pltpu
from jax.sharding import PartitionSpec as P

G = 256
DOMX, DOMY = 8, 16
SPANX, SPANY = 32, 16
PADY = 19
MAIN = PADY * SPANX
RIM = 24
N = DOMX * DOMY
ATOM_DEV = 1024
LANES = 768
HALFTILE = 640
CELLS = 704
TILES = LANES // 128
SELFS, PAIRS = 4, 62
REPS = 72
HALF = G
ewald_beta = 0.6
field_scale = 1.0
MESH = pl.DeviceIdType.MESH
f32, bf16 = jnp.float32, jnp.bfloat16


def side_by_side(table):
    high, low = halves(table)
    return np.block([[high, high], [low, np.zeros_like(low)]])


def halves(table):
    high = table.astype(ml_dtypes.bfloat16)
    low = (table - high.astype(np.float64)).astype(ml_dtypes.bfloat16)
    return high, low


def lane_cells():
    lane = np.arange(LANES)
    lane = np.where(lane < CELLS, lane, lane - (CELLS - HALFTILE))
    rim = np.maximum(lane - MAIN, 0)
    x = np.where(lane < MAIN, lane % SPANX, SPANX + rim // RIM)
    y = np.where(lane < MAIN, lane // SPANX, rim % RIM)
    return x, y, (x < SPANX + 3) & (y < PADY)


def self_and_pairs(first, second):
    selfs, pairs, seen = [], [], set()
    for a in range(first):
        for b in range(second):
            if (a, b) in seen:
                continue
            mirror = ((-a) % first, (-b) % second)
            seen.update([(a, b), mirror])
            (selfs if mirror == (a, b) else pairs).append((a, b))
    return selfs, pairs


def modulus(k):
    return 9.0 / (2.0 + np.cos(2.0 * np.pi * k / G)) ** 2


def signed(k):
    return np.where(k < G // 2, k, k - G).astype(np.float64)


def tables():
    out = {}
    wave = np.arange(G // 2)
    grid = np.arange(G)
    turn = 2.0 * np.pi / G
    first = np.cos(turn * (wave[:, None] * grid[None, :] % G))
    second = np.sin(turn * (wave[:, None] * grid[None, :] % G))
    second[0] = np.cos(np.pi * grid)
    out["basis"] = np.concatenate([first, second])

    x, y, valid = lane_cells()
    selfs, pairs = self_and_pairs(DOMX, DOMY)
    reps = selfs + pairs
    weight = np.array([1.0] * SELFS + [2.0] * PAIRS)
    kap = np.array([a for a, b in reps])
    lam = np.array([b for a, b in reps])
    source = np.arange(N)
    c, e = source // DOMY, source % DOMY
    steps = (2 * kap[:, None] * c[None, :] + lam[:, None] * e[None, :]) % 16
    angle = 2.0 * np.pi / 16 * steps
    left = np.zeros((2, REPS, N))
    left[0, : len(reps)] = np.cos(angle)
    left[1, : len(reps)] = np.where(steps % 8 == 0, 0.0, -np.sin(angle))
    kept = np.r_[0 : len(reps), REPS + SELFS : REPS + len(reps)]
    left = left.reshape(2 * REPS, N)
    out["left"], out["left_back"] = left, left[kept].T

    phase = turn * ((kap[:, None] * x[None, :] + lam[:, None] * y[None, :]) % G)
    lane = np.arange(LANES)
    twiddle = np.zeros((2, 2, REPS, LANES))
    for j, kept in enumerate((lane < CELLS, (lane < HALFTILE) | (lane >= CELLS))):
        twiddle[j, 0, : len(reps)] = np.cos(phase) * (valid & kept)
        twiddle[j, 1, : len(reps)] = np.sin(phase) * (valid & kept)
    out["twiddle"] = twiddle

    selfs_in, pairs_in = self_and_pairs(SPANX, SPANY)
    plus = pairs_in + selfs_in[:2]
    minus = [((-a) % SPANX, (-b) % SPANY) for a, b in pairs_in] + selfs_in[2:]

    def inner(modes):
        m = np.array([a for a, b in modes])
        n = np.array([b for a, b in modes])
        return 2.0 * np.pi / 32 * ((x[:, None] * m[None, :] + 2 * y[:, None] * n[None, :]) % 32)

    right = np.concatenate(
        [
            np.cos(inner(plus)),
            np.sin(inner(pairs_in)),
            np.cos(inner(selfs_in[2:])),
        ],
        axis=1,
    )
    out["right"] = right * valid[:, None]
    out["right_back"] = out["right"].T

    rate = (np.pi / (ewald_beta * G)) ** 2
    bump = np.zeros((4, REPS, HALF))
    bump[2:] = 1.0
    for row, modes in enumerate((plus, minus)):
        kx = kap[:, None] + DOMX * np.array([a for a, b in modes])[None, :]
        ky = lam[:, None] + DOMY * np.array([b for a, b in modes])[None, :]
        square = signed(kx) ** 2 + signed(ky) ** 2
        bump[row, : len(reps)] = weight[:, None] * modulus(kx) * modulus(ky) * np.exp(-rate * square)
        bump[2 + row, : len(reps)] = square
    out["bump"] = bump

    strength = field_scale * G**3.5 / math.sqrt(N * ATOM_DEV)
    along = np.zeros((N, 128))
    for j in range(2):
        k = wave.copy()
        share = np.full(N, 2.0)
        share[0] = 1.0
        if j == 1:
            k[0] = G // 2
        square = signed(k) ** 2
        along[:, j] = strength * modulus(k) * np.exp(-rate * square) * share / float(G) ** 3
        along[:, 2 + j] = square
    out["along"] = along
    return out


def far_first():
    hops = (0, 1, 2, 1)
    offsets = [(y, x, c, z) for y in range(4) for x in range(4) for c in range(2) for z in range(4)]
    spread_out = np.random.RandomState(1).permutation(len(offsets))
    offsets = [offsets[k] for k in spread_out if any(offsets[k])]
    return sorted(offsets, key=lambda o: -(hops[o[0]] + hops[o[1]] + hops[o[3]]))


def split(value):
    high = value.astype(bf16)
    return high, (value - high.astype(f32)).astype(bf16)


def dot3(a, b, dims=((1,), (0,))):
    def one(p, q):
        return lax.dot_general(p, q, (dims, ((), ())), preferred_element_type=f32)

    return one(a[0], b[0]) + (one(a[0], b[1]) + one(a[1], b[0]))


def dot(a, b):
    return jnp.dot(a, b, preferred_element_type=f32)


def splines(u):
    rest = 1.0 - u
    square = u * u
    cube = square * u
    values = [
        rest * rest * rest / 6.0,
        (3.0 * cube - 6.0 * square + 4.0) / 6.0,
        (-3.0 * cube + 3.0 * square + 3.0 * u + 1.0) / 6.0,
        cube / 6.0,
    ]
    slopes = [
        -0.5 * rest * rest,
        0.5 * (3.0 * square - 4.0 * u),
        0.5 * (-3.0 * square + 2.0 * u + 1.0),
        0.5 * square,
    ]
    return values, slopes


def spread(rows, first, terms, wrap=None):
    shape = (rows, first.shape[1])
    offset = lax.broadcasted_iota(jnp.int32, shape, 0) - first
    if wrap:
        offset = offset & (wrap - 1)
    masks = [offset == a for a in range(4)]
    outs = []
    for term in terms:
        total = jnp.where(masks[3], term[3], 0.0)
        for a in (2, 1, 0):
            total = jnp.where(masks[a], term[a], total)
        outs.append(total)
    return outs


def body(
    charges_any, fractions_any, bases_any, counts, basis_any, left_any, back_any, right_any, wide_any, twiddle_any,
    bump_any, along_any, out, basis, left, left_back, right, right_back, twiddle, bump, along,
    charges, fractions, bases, tw, bt, send_a, send_b, recv_a, recv_b,
    back_a, back_b, home_a, home_b, gt, early, sems, loads,
):
    dom, z = lax.axis_index("dom"), lax.axis_index("grid")
    p = dom * 4 + z
    barrier = pltpu.get_barrier_semaphore()
    loading = [
        pltpu.make_async_copy(source, target, loads.at[k])
        for k, (source, target) in enumerate(
            (
                (fractions_any, fractions), (bases_any, bases), (charges_any, charges), (basis_any, basis),
                (left_any, left), (right_any, right), (twiddle_any, twiddle), (wide_any, right_back),
                (bump_any, bump), (along_any, along), (back_any, left_back),
            )
        )
    ]
    for load in loading:
        load.start()

    ys = [lax.rem(dom // 8 + k, 4) * 8 for k in range(4)]
    xs = [lax.rem(lax.rem(dom, 8) // 2 + k, 4) * 2 for k in range(4)]
    cores = [lax.rem(dom + k, 2) for k in range(2)]
    zs = [lax.rem(z + k, 4) for k in range(4)]
    chips = [[a + b for b in xs] for a in ys]
    peers = [(chips[a][b] + cores[c], zs[k]) for a, b, c, k in far_first()]

    for where in peers:
        pl.semaphore_signal(barrier, inc=1, device_id=where, device_id_type=MESH)

    def post(source, target, which):
        for where in peers:
            pltpu.make_async_remote_copy(
                src_ref=source.at[where[0] * 4 + where[1]], dst_ref=target.at[p],
                send_sem=sems.at[2 * which], recv_sem=sems.at[2 * which + 1],
                device_id=where, device_id_type=MESH,
            ).start()
        target[pl.ds(p, 1)] = source[pl.ds(p, 1)]

    def every(source, target, which):
        return pltpu.make_async_remote_copy(
            src_ref=source.at[pl.ds(0, N - 1)], dst_ref=target.at[pl.ds(0, N - 1)],
            send_sem=sems.at[2 * which], recv_sem=sems.at[2 * which + 1],
            device_id=peers[0], device_id_type=MESH,
        )

    for load in loading[:3]:
        load.wait()
    values, slopes = splines(fractions[...])
    alive = lax.broadcasted_iota(jnp.int32, (1, ATOM_DEV), 1) < counts[0]
    weighted = jnp.where(alive, charges[...], 0.0)

    def row(which, terms):
        return [t[which : which + 1] for t in terms]

    (wz,) = spread(G, bases[2:3], (row(2, values),), G)
    wz = split(wz)
    loading[3].wait()
    high, low = split(dot3((basis[0], basis[1]), wz))
    tw[0, 0] = high
    tw[1, 0] = low

    local_x = bases[0:1] - (p // DOMY) * SPANX
    local_y = bases[1:2] - lax.rem(p, DOMY) * SPANY
    wx, sx = spread(40, local_x, (row(0, values), row(0, slopes)))
    wy, sy = spread(RIM, local_y, (row(1, values), row(1, slopes)))
    charged = wx * weighted
    for y in range(PADY):
        high, low = split(charged[:SPANX] * wy[y : y + 1])
        bt[0, pl.ds(y * SPANX, SPANX)] = high
        bt[1, pl.ds(y * SPANX, SPANX)] = low
    rim = [charged[SPANX + a : SPANX + a + 1] * wy for a in range(3)]
    high, low = split(jnp.concatenate(rim + [jnp.zeros((CELLS - MAIN - 3 * RIM, ATOM_DEV), f32)], axis=0))
    for k, part in enumerate((high, low)):
        bt[k, pl.ds(MAIN, CELLS - MAIN)] = part

    planes = dot3((tw[0, 0], tw[1, 0]), (bt[0], bt[1]), ((1,), (1,)))

    def put(target, value, tiles):
        for t in range(tiles):
            target[:, t, :] = value[:, t * 128 : (t + 1) * 128]

    put(send_a, planes[:N], TILES - 1)
    put(send_b, planes[N:], TILES - 1)
    send_a[:, TILES - 1, :] = jnp.concatenate([planes[:N, HALFTILE:], planes[N:, HALFTILE:]], axis=1)
    pl.semaphore_wait(barrier, N - 1)
    post(send_a, recv_a, 0)

    (sz,) = spread(G, bases[2:3], (row(2, slopes),), G)
    high, low = split(dot3((basis[0], basis[1]), split(sz)))
    tw[0, 1] = high
    tw[1, 1] = low
    post(send_b, recv_b, 1)
    for load in loading[4:]:
        load.wait()
    mine = along[pl.ds(p, 1), :]
    lane = lax.broadcasted_iota(jnp.int32, (REPS, HALF), 1)
    paired = lane < HALF - 2
    factors = []
    for j in range(2):
        scale, square = mine[:, j : j + 1], mine[:, 2 + j : 3 + j]
        both = []
        for end in range(2):
            whole = bump[2 + end] + square
            positive = whole > 0.0
            both.append(
                jnp.where(positive, bump[end] * scale / jnp.where(positive, whole, 1.0), 0.0)
            )
        total = both[0] + both[1]
        factors.append(
            (
                jnp.where(paired, total, both[0]),
                jnp.where(paired, total, both[1]),
                jnp.where(paired, both[0] - both[1], 0.0),
            )
        )

    def filtered(tiles, j):
        high, low = split(jnp.concatenate(tiles, axis=1))
        first = dot(left[...], jnp.concatenate([high, low], axis=0))
        first = first[: 2 * REPS] + first[2 * REPS :]
        real, imag = first[:REPS], first[REPS:]
        tc, ts = twiddle[j, 0], twiddle[j, 1]
        turned = jnp.concatenate([real * tc + imag * ts, imag * tc - real * ts], axis=0)
        wide = (right[0], right[1])
        modes = dot3(split(turned), wide)
        f1, f2, fd = factors[j]
        rc, rs = modes[:REPS, :HALF], modes[:REPS, HALF:]
        ic, is_ = modes[REPS:, :HALF], modes[REPS:, HALF:]
        modes = jnp.concatenate(
            [
                jnp.concatenate([f1 * rc + fd * is_, f2 * rs - fd * ic], axis=1),
                jnp.concatenate([f1 * ic - fd * rs, fd * rc + f2 * is_], axis=1),
            ],
            axis=0,
        )
        cells = dot3(split(modes), (right_back[0], right_back[1]))
        real, imag = cells[:REPS], cells[REPS:]
        turned = jnp.concatenate(
            [(real * tc - imag * ts)[: SELFS + PAIRS], (imag * tc + real * ts)[SELFS : SELFS + PAIRS]],
            axis=0,
        )
        both = dot(left_back[...], jnp.concatenate(split(turned), axis=0))
        return both[:N] + both[N:]

    every(send_a, recv_a, 0).wait_recv()
    plane = filtered([recv_a[:, t, :] for t in range(TILES)], 0)
    put(back_a, plane, TILES - 1)
    back_b[:, TILES - 1, :] = plane[:, HALFTILE:]
    post(back_a, home_a, 2)
    every(send_b, recv_b, 1).wait_recv()
    plane = filtered([recv_b[:, t, :] for t in range(TILES - 1)] + [recv_a[:, TILES - 1, :]], 1)
    put(back_b, plane, TILES - 1)
    back_b[:, TILES - 1, :] += plane[:, HALFTILE:]
    post(back_b, home_b, 3)

    every(send_a, recv_a, 0).wait_send()
    every(send_b, recv_b, 1).wait_send()
    chunk = 256

    def fold(part):
        return sum(part[8 * i : 8 * i + 8] for i in range(1, part.shape[0] // 8)) + part[:8]

    def gather(here, field, slope):
        sums = [jnp.zeros((8, chunk), f32) for _ in range(3)]
        for y in range(PADY):
            cells = slice(y * SPANX, (y + 1) * SPANX)
            inner = fold(field[cells] * wx[:SPANX, here])
            sums[0] += fold(field[cells] * sx[:SPANX, here]) * wy[y : y + 1, here]
            sums[1] += inner * sy[y : y + 1, here]
            sums[2] += fold(slope[cells] * wx[:SPANX, here]) * wy[y : y + 1, here]
        for a in range(3):
            cells = slice(MAIN + a * RIM, min(MAIN + (a + 1) * RIM, field.shape[0]))
            if cells.start >= field.shape[0]:
                continue
            x = slice(SPANX + a, SPANX + a + 1)
            rows = slice(0, cells.stop - cells.start)
            sums[0] += fold(field[cells] * wy[rows, here]) * sx[x, here]
            sums[1] += fold(field[cells] * sy[rows, here]) * wx[x, here]
            sums[2] += fold(slope[cells] * wy[rows, here]) * wx[x, here]
        return sums

    def gather_tail(sums, here, field, slope):
        for row in range(HALFTILE, MAIN + 3 * RIM, 8):
            a, y = (row - MAIN) // RIM, (row - MAIN) % RIM
            x, rows = slice(SPANX + a, SPANX + a + 1), slice(y, y + 8)
            cells = slice(row - HALFTILE, row - HALFTILE + 8)
            sums[0] += field[cells] * wy[rows, here] * sx[x, here]
            sums[1] += field[cells] * sy[rows, here] * wx[x, here]
            sums[2] += slope[cells] * wy[rows, here] * wx[x, here]

    def columns(j, part, here):
        rows = slice(j * N, (j + 1) * N)
        high = tw[0, part, rows, here]
        return jnp.concatenate([high, high], axis=0), tw[1, part, rows, here]

    def fields(j, part, here):
        twice, low = columns(j, part, here)
        return dot(gt[j, :HALFTILE], twice) + dot(gt[j, :HALFTILE, :N], low)

    def turn(home, j):
        for t in range(TILES - 1):
            rows = pl.ds(t * 128, 128)
            gt[j, rows, :N], gt[j, rows, N:] = split(home[:, t, :].T)

    chunks = [slice(r, r + chunk) for r in range(0, ATOM_DEV, chunk)]
    every(back_a, home_a, 2).wait_recv()
    turn(home_a, 0)
    for here in chunks:
        for a, part in enumerate(gather(here, fields(0, 0, here), fields(0, 1, here))):
            early[a, :, here] = part
    every(back_b, home_b, 3).wait_recv()
    turn(home_b, 1)
    shared = home_b[:, TILES - 1, :].T
    shared = split(jnp.concatenate([shared[:64], shared[64:]], axis=1))
    for here in chunks:
        sums = gather(here, fields(1, 0, here), fields(1, 1, here))
        tails = [dot3(shared, (tw[0, k, :, here], tw[1, k, :, here])) for k in range(2)]
        gather_tail(sums, here, *tails)
        for a in range(3):
            total = jnp.sum(sums[a] + early[a, :, here], axis=0, keepdims=True)
            out[a : a + 1, here] = -weighted[:, here] * total
    every(back_a, home_a, 2).wait_send()
    every(back_b, home_b, 3).wait_send()


def solution(mesh):
    table = tables()
    pairs = {k: np.stack(halves(table[k])) for k in ("basis", "right", "right_back")}
    pairs.update({k: side_by_side(table[k]) for k in ("left", "left_back")})
    plain = {k: table[k].astype(np.float32) for k in ("twiddle", "bump", "along")}
    held = [pairs[k] for k in ("basis", "left", "left_back", "right", "right_back")]
    held += [plain["twiddle"], plain["bump"], plain["along"]]
    vmem = pl.BlockSpec(memory_space=pltpu.VMEM)
    smem = pl.BlockSpec(memory_space=pltpu.SMEM)
    anywhere = pl.BlockSpec(memory_space=pl.ANY)
    five, six = (pltpu.VMEM((N, rows, 128), f32) for rows in (TILES - 1, TILES))
    call = pl.pallas_call(
        body,
        out_shape=jax.ShapeDtypeStruct((3, ATOM_DEV), f32),
        in_specs=[anywhere] * 3 + [smem] + [anywhere] * 8,
        out_specs=vmem,
        scratch_shapes=[pltpu.VMEM(a.shape, bf16 if a.dtype != np.float32 else f32) for a in held]
        + [
            pltpu.VMEM((1, ATOM_DEV), f32),
            pltpu.VMEM((3, ATOM_DEV), f32),
            pltpu.VMEM((3, ATOM_DEV), jnp.int32),
            pltpu.VMEM((2, 2, G, ATOM_DEV), bf16),
            pltpu.VMEM((2, CELLS, ATOM_DEV), bf16),
            six, five, six, five,
            five, six, five, six,
            pltpu.VMEM((2, HALFTILE, G), bf16),
            pltpu.VMEM((3, 8, ATOM_DEV), f32),
            pltpu.SemaphoreType.DMA((8,)),
            pltpu.SemaphoreType.DMA((11,)),
        ],
        compiler_params=pltpu.CompilerParams(
            collective_id=1, has_side_effects=True, vmem_limit_bytes=56 << 20
        ),
    )

    def local(charges, fractions, bases, counts):
        return call(
            charges.reshape(1, ATOM_DEV), fractions, bases, counts, *held
        )

    placed = (
        P(("dom", "grid")),
        P(None, ("dom", "grid")),
        P(None, ("dom", "grid")),
        P(("dom", "grid")),
    )
    return jax.shard_map(
        local, mesh=mesh, in_specs=placed, out_specs=P(None, ("dom", "grid")), check_vma=False
    )
```

```python
import functools
import math

import jax
import jax.numpy as jnp
import numpy as np
import ml_dtypes
from jax import lax
from jax.experimental import pallas as pl
from jax.experimental.pallas import tpu as pltpu
from jax.sharding import PartitionSpec as P

G = 256
DOMX, DOMY = 8, 16
SPANX, SPANY = 32, 16
PADY = 19
MAIN = PADY * SPANX
RIM = 24
N = DOMX * DOMY
ATOM_DEV = 1024
LANES = 768
HALFTILE = 640
CELLS = 704
TILES = LANES // 128
SELFS, PAIRS = 4, 62
REPS = 72
HALF = G
ewald_beta = 0.6
field_scale = 1.0
MESH = pl.DeviceIdType.MESH
f32, bf16 = jnp.float32, jnp.bfloat16


def side_by_side(table):
    high, low = halves(table)
    return np.concatenate([high, low, high], axis=1)


def halves(table):
    high = table.astype(ml_dtypes.bfloat16)
    low = (table - high.astype(np.float64)).astype(ml_dtypes.bfloat16)
    return high, low


def lane_cells():
    lane = np.arange(LANES)
    lane = np.where(lane < CELLS, lane, lane - (CELLS - HALFTILE))
    rim = np.maximum(lane - MAIN, 0)
    x = np.where(lane < MAIN, lane % SPANX, SPANX + rim // RIM)
    y = np.where(lane < MAIN, lane // SPANX, rim % RIM)
    return x, y, (x < SPANX + 3) & (y < PADY)


def self_and_pairs(first, second):
    selfs, pairs, seen = [], [], set()
    for a in range(first):
        for b in range(second):
            if (a, b) in seen:
                continue
            mirror = ((-a) % first, (-b) % second)
            seen.update([(a, b), mirror])
            (selfs if mirror == (a, b) else pairs).append((a, b))
    return selfs, pairs


def modulus(k):
    return 9.0 / (2.0 + np.cos(2.0 * np.pi * k / G)) ** 2


def signed(k):
    return np.where(k < G // 2, k, k - G).astype(np.float64)


def tables():
    out = {}
    wave = np.arange(G // 2)
    grid = np.arange(G)
    turn = 2.0 * np.pi / G
    first = np.cos(turn * (wave[:, None] * grid[None, :] % G))
    second = np.sin(turn * (wave[:, None] * grid[None, :] % G))
    second[0] = np.cos(np.pi * grid)
    out["basis"] = np.concatenate([first, second])

    x, y, valid = lane_cells()
    selfs, pairs = self_and_pairs(DOMX, DOMY)
    reps = selfs + pairs
    weight = np.array([1.0] * SELFS + [2.0] * PAIRS)
    kap = np.array([a for a, b in reps])
    lam = np.array([b for a, b in reps])
    source = np.arange(N)
    c, e = source // DOMY, source % DOMY
    steps = (2 * kap[:, None] * c[None, :] + lam[:, None] * e[None, :]) % 16
    angle = 2.0 * np.pi / 16 * steps
    left = np.zeros((2, REPS, N))
    left[0, : len(reps)] = np.cos(angle)
    left[1, : len(reps)] = np.where(steps % 8 == 0, 0.0, -np.sin(angle))
    kept = np.r_[0 : len(reps), REPS + SELFS : REPS + len(reps)]
    left = left.reshape(2 * REPS, N)
    out["left"], out["left_back"] = left, left[kept].T

    phase = turn * ((kap[:, None] * x[None, :] + lam[:, None] * y[None, :]) % G)
    lane = np.arange(LANES)
    twiddle = np.zeros((2, 2, REPS, LANES))
    for j, kept in enumerate((lane < CELLS, (lane < HALFTILE) | (lane >= CELLS))):
        twiddle[j, 0, : len(reps)] = np.cos(phase) * (valid & kept)
        twiddle[j, 1, : len(reps)] = np.sin(phase) * (valid & kept)
    out["twiddle"] = twiddle

    selfs_in, pairs_in = self_and_pairs(SPANX, SPANY)
    plus = pairs_in + selfs_in[:2]
    minus = [((-a) % SPANX, (-b) % SPANY) for a, b in pairs_in] + selfs_in[2:]

    def inner(modes):
        m = np.array([a for a, b in modes])
        n = np.array([b for a, b in modes])
        return 2.0 * np.pi / 32 * ((x[:, None] * m[None, :] + 2 * y[:, None] * n[None, :]) % 32)

    right = np.concatenate(
        [
            np.cos(inner(plus)),
            np.sin(inner(pairs_in)),
            np.cos(inner(selfs_in[2:])),
        ],
        axis=1,
    )
    out["right"] = right * valid[:, None]
    out["right_back"] = out["right"].T

    rate = (np.pi / (ewald_beta * G)) ** 2
    bump = np.zeros((4, REPS, HALF))
    bump[2:] = 1.0
    for row, modes in enumerate((plus, minus)):
        kx = kap[:, None] + DOMX * np.array([a for a, b in modes])[None, :]
        ky = lam[:, None] + DOMY * np.array([b for a, b in modes])[None, :]
        square = signed(kx) ** 2 + signed(ky) ** 2
        bump[row, : len(reps)] = weight[:, None] * modulus(kx) * modulus(ky) * np.exp(-rate * square)
        bump[2 + row, : len(reps)] = square
    out["bump"] = bump

    strength = field_scale * G**3.5 / math.sqrt(N * ATOM_DEV)
    along = np.zeros((N, 128))
    for j in range(2):
        k = wave.copy()
        share = np.full(N, 2.0)
        share[0] = 1.0
        if j == 1:
            k[0] = G // 2
        square = signed(k) ** 2
        along[:, j] = strength * modulus(k) * np.exp(-rate * square) * share / float(G) ** 3
        along[:, 2 + j] = square
    out["along"] = along
    return out


def far_first():
    hops = (0, 1, 2, 1)
    offsets = [(y, x, c, z) for y in range(4) for x in range(4) for c in range(2) for z in range(4)]
    spread_out = np.random.RandomState(1).permutation(len(offsets))
    offsets = [offsets[k] for k in spread_out if any(offsets[k])]
    return sorted(offsets, key=lambda o: -(hops[o[0]] + hops[o[1]] + hops[o[3]]))


def split(value):
    high = value.astype(bf16)
    return high, (value - high.astype(f32)).astype(bf16)


def dot3(a, b, across=0):
    left = jnp.concatenate([a[0], a[1], a[0]], axis=1)
    right = jnp.concatenate([b[0], b[0], b[1]], axis=across)
    return lax.dot_general(left, right, (((1,), (across,)), ((), ())), preferred_element_type=f32)


def dot(a, b):
    return jnp.dot(a, b, preferred_element_type=f32)


def splines(u):
    rest = 1.0 - u
    square = u * u
    cube = square * u
    values = [
        rest * rest * rest / 6.0,
        (3.0 * cube - 6.0 * square + 4.0) / 6.0,
        (-3.0 * cube + 3.0 * square + 3.0 * u + 1.0) / 6.0,
        cube / 6.0,
    ]
    slopes = [
        -0.5 * rest * rest,
        0.5 * (3.0 * square - 4.0 * u),
        0.5 * (-3.0 * square + 2.0 * u + 1.0),
        0.5 * square,
    ]
    return values, slopes


def spread(rows, first, terms, wrap=None):
    shape = (rows, first.shape[1])
    offset = lax.broadcasted_iota(jnp.int32, shape, 0) - first
    if wrap:
        offset = offset & (wrap - 1)
    masks = [offset == a for a in range(4)]
    outs = []
    for term in terms:
        total = jnp.where(masks[3], term[3], 0.0)
        for a in (2, 1, 0):
            total = jnp.where(masks[a], term[a], total)
        outs.append(total)
    return outs


def body(
    charges_any, fractions_any, bases_any, counts, basis_any, left_any, back_any, right_any, wide_any, twiddle_any,
    bump_any, along_any, out, basis, left, left_back, right, right_back, twiddle, bump, along,
    charges, fractions, bases, tw, bt, send_a, send_b, recv_a, recv_b,
    back_a, back_b, home_a, home_b, gt, early, sems, loads,
):
    dom, z = lax.axis_index("dom"), lax.axis_index("grid")
    p = dom * 4 + z
    barrier = pltpu.get_barrier_semaphore()
    loading = [
        pltpu.make_async_copy(source, target, loads.at[k])
        for k, (source, target) in enumerate(
            (
                (fractions_any, fractions), (bases_any, bases), (charges_any, charges), (basis_any, basis),
                (left_any, left), (right_any, right), (twiddle_any, twiddle), (wide_any, right_back),
                (bump_any, bump), (along_any, along), (back_any, left_back),
            )
        )
    ]
    for load in loading:
        load.start()

    ys = [lax.rem(dom // 8 + k, 4) * 8 for k in range(4)]
    xs = [lax.rem(lax.rem(dom, 8) // 2 + k, 4) * 2 for k in range(4)]
    cores = [lax.rem(dom + k, 2) for k in range(2)]
    zs = [lax.rem(z + k, 4) for k in range(4)]
    chips = [[a + b for b in xs] for a in ys]
    peers = [(chips[a][b] + cores[c], zs[k]) for a, b, c, k in far_first()]

    for where in peers:
        pl.semaphore_signal(barrier, inc=1, device_id=where, device_id_type=MESH)

    def post(source, target, which):
        for where in peers:
            pltpu.make_async_remote_copy(
                src_ref=source.at[pl.ds(where[0] * 4 + where[1], 1)], dst_ref=target.at[pl.ds(p, 1)],
                send_sem=sems.at[2 * which], recv_sem=sems.at[2 * which + 1],
                device_id=where, device_id_type=MESH,
            ).start()
        pltpu.make_async_copy(
            source.at[pl.ds(p, 1)], target.at[pl.ds(p, 1)], sems.at[2 * which + 1]
        ).start()

    def arrived(target, which):
        pltpu.make_async_copy(target, target, sems.at[2 * which + 1]).wait()

    def sent(source, which):
        for first, rows in [(0, N - 8)] + [(k, 1) for k in range(N - 8, N - 1)]:
            part = source.at[pl.ds(first, rows)]
            pltpu.make_async_copy(part, part, sems.at[2 * which]).wait()

    for load in loading[:3]:
        load.wait()
    values, slopes = splines(fractions[...])
    alive = lax.broadcasted_iota(jnp.int32, (1, ATOM_DEV), 1) < counts[0]
    weighted = jnp.where(alive, charges[...], 0.0)

    def row(which, terms):
        return [t[which : which + 1] for t in terms]

    (wz,) = spread(G, bases[2:3], (row(2, values),), G)
    wz = split(wz)
    loading[3].wait()
    high, low = split(dot3((basis[0], basis[1]), wz))
    tw[0, 0] = high
    tw[1, 0] = low

    local_x = bases[0:1] - (p // DOMY) * SPANX
    local_y = bases[1:2] - lax.rem(p, DOMY) * SPANY
    wx, sx = spread(40, local_x, (row(0, values), row(0, slopes)))
    wy, sy = spread(RIM, local_y, (row(1, values), row(1, slopes)))
    charged = wx * weighted
    for y in range(PADY):
        high, low = split(charged[:SPANX] * wy[y : y + 1])
        bt[0, pl.ds(y * SPANX, SPANX)] = high
        bt[1, pl.ds(y * SPANX, SPANX)] = low
    rim = [charged[SPANX + a : SPANX + a + 1] * wy for a in range(3)]
    high, low = split(jnp.concatenate(rim + [jnp.zeros((CELLS - MAIN - 3 * RIM, ATOM_DEV), f32)], axis=0))
    for k, part in enumerate((high, low)):
        bt[k, pl.ds(MAIN, CELLS - MAIN)] = part

    planes = dot3((tw[0, 0], tw[1, 0]), (bt[0], bt[1]), 1)

    send_a[:, :HALFTILE] = planes[:N, :HALFTILE]
    send_b[...] = planes[N:, :HALFTILE]
    send_a[:, HALFTILE:] = jnp.concatenate([planes[:N, HALFTILE:], planes[N:, HALFTILE:]], axis=1)
    pl.semaphore_wait(barrier, N - 1)
    post(send_a, recv_a, 0)

    (sz,) = spread(G, bases[2:3], (row(2, slopes),), G)
    high, low = split(dot3((basis[0], basis[1]), split(sz)))
    tw[0, 1] = high
    tw[1, 1] = low
    post(send_b, recv_b, 1)
    for load in loading[4:]:
        load.wait()
    mine = along[pl.ds(p, 1), :]
    lane = lax.broadcasted_iota(jnp.int32, (REPS, HALF), 1)
    paired = lane < HALF - 2
    factors = []
    for j in range(2):
        scale, square = mine[:, j : j + 1], mine[:, 2 + j : 3 + j]
        both = []
        for end in range(2):
            whole = bump[2 + end] + square
            positive = whole > 0.0
            both.append(
                jnp.where(positive, bump[end] * scale / jnp.where(positive, whole, 1.0), 0.0)
            )
        total = both[0] + both[1]
        factors.append(
            (
                jnp.where(paired, total, both[0]),
                jnp.where(paired, total, both[1]),
                jnp.where(paired, both[0] - both[1], 0.0),
            )
        )

    def filtered(arrival, j):
        high, low = split(arrival)
        first = dot(left[...], jnp.concatenate([high, high, low], axis=0))
        real, imag = first[:REPS], first[REPS:]
        tc, ts = twiddle[j, 0], twiddle[j, 1]
        turned = jnp.concatenate([real * tc + imag * ts, imag * tc - real * ts], axis=0)
        wide = (right[0], right[1])
        modes = dot3(split(turned), wide)
        f1, f2, fd = factors[j]
        rc, rs = modes[:REPS, :HALF], modes[:REPS, HALF:]
        ic, is_ = modes[REPS:, :HALF], modes[REPS:, HALF:]
        modes = jnp.concatenate(
            [
                jnp.concatenate([f1 * rc + fd * is_, f2 * rs - fd * ic], axis=1),
                jnp.concatenate([f1 * ic - fd * rs, fd * rc + f2 * is_], axis=1),
            ],
            axis=0,
        )
        cells = dot3(split(modes), (right_back[0], right_back[1]))
        real, imag = cells[:REPS], cells[REPS:]
        turned = jnp.concatenate(
            [(real * tc - imag * ts)[: SELFS + PAIRS], (imag * tc + real * ts)[SELFS : SELFS + PAIRS]],
            axis=0,
        )
        high, low = split(turned)
        return dot(left_back[...], jnp.concatenate([high, high, low], axis=0))

    arrived(recv_a, 0)
    plane = filtered(recv_a[...], 0)
    back_a[...] = plane[:, :HALFTILE]
    back_b[:, HALFTILE:] = plane[:, HALFTILE:]
    post(back_a, home_a, 2)
    arrived(recv_b, 1)
    plane = filtered(jnp.concatenate([recv_b[...], recv_a[:, HALFTILE:]], axis=1), 1)
    back_b[:, :HALFTILE] = plane[:, :HALFTILE]
    back_b[:, HALFTILE:] += plane[:, HALFTILE:]
    post(back_b, home_b, 3)

    sent(send_a, 0)
    sent(send_b, 1)
    chunk = 256

    def fold(part):
        return sum(part[8 * i : 8 * i + 8] for i in range(1, part.shape[0] // 8)) + part[:8]

    def gather(here, field, slope):
        sums = [jnp.zeros((8, chunk), f32) for _ in range(3)]
        for y in range(PADY):
            cells = slice(y * SPANX, (y + 1) * SPANX)
            inner = fold(field[cells] * wx[:SPANX, here])
            sums[0] += fold(field[cells] * sx[:SPANX, here]) * wy[y : y + 1, here]
            sums[1] += inner * sy[y : y + 1, here]
            sums[2] += fold(slope[cells] * wx[:SPANX, here]) * wy[y : y + 1, here]
        for a in range(3):
            cells = slice(MAIN + a * RIM, min(MAIN + (a + 1) * RIM, field.shape[0]))
            if cells.start >= field.shape[0]:
                continue
            x = slice(SPANX + a, SPANX + a + 1)
            rows = slice(0, cells.stop - cells.start)
            sums[0] += fold(field[cells] * wy[rows, here]) * sx[x, here]
            sums[1] += fold(field[cells] * sy[rows, here]) * wx[x, here]
            sums[2] += fold(slope[cells] * wy[rows, here]) * wx[x, here]
        return sums

    def gather_tail(sums, here, field, slope):
        for row in range(HALFTILE, MAIN + 3 * RIM, 8):
            a, y = (row - MAIN) // RIM, (row - MAIN) % RIM
            x, rows = slice(SPANX + a, SPANX + a + 1), slice(y, y + 8)
            cells = slice(row - HALFTILE, row - HALFTILE + 8)
            sums[0] += field[cells] * wy[rows, here] * sx[x, here]
            sums[1] += field[cells] * sy[rows, here] * wx[x, here]
            sums[2] += slope[cells] * wy[rows, here] * wx[x, here]

    def fields(j, part, here):
        rows = slice(j * N, (j + 1) * N)
        high = tw[0, part, rows, here]
        parts = [high, high, tw[1, part, rows, here]]
        if j == 0:
            return dot(gt[0, :HALFTILE, : 3 * N], jnp.concatenate(parts, axis=0))
        other = tw[0, part, :N, here]
        whole = dot(gt[1], jnp.concatenate(parts + [other], axis=0))
        rest = dot(gt[0, HALFTILE:, : 2 * N], jnp.concatenate([other, tw[1, part, :N, here]], axis=0))
        return whole[:HALFTILE], whole[HALFTILE:] + rest

    def turn(home, j):
        for t in range(TILES - 1):
            rows = pl.ds(t * 128, 128)
            high, low = split(home[:, t * 128 : (t + 1) * 128].T)
            gt[j, rows] = jnp.concatenate([high, low, high, jnp.zeros_like(high)], axis=1)

    chunks = [slice(r, r + chunk) for r in range(0, ATOM_DEV, chunk)]
    arrived(home_a, 2)
    turn(home_a, 0)
    for here in chunks:
        for a, part in enumerate(gather(here, fields(0, 0, here), fields(0, 1, here))):
            early[a, :, here] = part
    arrived(home_b, 3)
    turn(home_b, 1)
    shared = home_b[:, HALFTILE:].T
    (high, other), (low, least) = ((part[64:], part[:64]) for part in split(shared))
    gt[1, HALFTILE:] = jnp.concatenate([high, low, high, other], axis=1)
    gt[0, HALFTILE:, : 2 * N] = jnp.concatenate([least, other], axis=1)
    for here in chunks:
        (field, field_tail), (slope, slope_tail) = fields(1, 0, here), fields(1, 1, here)
        sums = gather(here, field, slope)
        gather_tail(sums, here, field_tail, slope_tail)
        for a in range(3):
            total = jnp.sum(sums[a] + early[a, :, here], axis=0, keepdims=True)
            out[a : a + 1, here] = -weighted[:, here] * total
    sent(back_a, 2)
    sent(back_b, 3)


def solution(mesh):
    table = tables()
    pairs = {k: np.stack(halves(table[k])) for k in ("basis", "right", "right_back")}
    pairs.update({k: side_by_side(table[k]) for k in ("left", "left_back")})
    plain = {k: table[k].astype(np.float32) for k in ("twiddle", "bump", "along")}
    held = [pairs[k] for k in ("basis", "left", "left_back", "right", "right_back")]
    held += [plain["twiddle"], plain["bump"], plain["along"]]
    vmem = pl.BlockSpec(memory_space=pltpu.VMEM)
    smem = pl.BlockSpec(memory_space=pltpu.SMEM)
    anywhere = pl.BlockSpec(memory_space=pl.ANY)
    five, six = (pltpu.VMEM((N, lanes), f32) for lanes in (HALFTILE, LANES))
    call = pl.pallas_call(
        body,
        out_shape=pltpu.VMEM((3, ATOM_DEV), f32),
        in_specs=[anywhere] * 3 + [smem] + [anywhere] * 8,
        out_specs=vmem,
        scratch_shapes=[pltpu.VMEM(a.shape, bf16 if a.dtype != np.float32 else f32) for a in held]
        + [
            pltpu.VMEM((1, ATOM_DEV), f32),
            pltpu.VMEM((3, ATOM_DEV), f32),
            pltpu.VMEM((3, ATOM_DEV), jnp.int32),
            pltpu.VMEM((2, 2, G, ATOM_DEV), bf16),
            pltpu.VMEM((2, CELLS, ATOM_DEV), bf16),
            six, five, six, five,
            five, six, five, six,
            pltpu.VMEM((2, CELLS, 4 * N), bf16),
            pltpu.VMEM((3, 8, ATOM_DEV), f32),
            pltpu.SemaphoreType.DMA((8,)),
            pltpu.SemaphoreType.DMA((11,)),
        ],
        compiler_params=pltpu.CompilerParams(
            collective_id=1, has_side_effects=True, vmem_limit_bytes=56 << 20
        ),
    )

    def local(charges, fractions, bases, counts):
        return call(
            charges.reshape(1, ATOM_DEV), fractions, bases, counts, *held
        )

    placed = (
        P(("dom", "grid")),
        P(None, ("dom", "grid")),
        P(None, ("dom", "grid")),
        P(("dom", "grid")),
    )
    return jax.shard_map(
        local, mesh=mesh, in_specs=placed, out_specs=P(None, ("dom", "grid")), check_vma=False
    )
```

```python
import functools
import math

import jax
import jax.numpy as jnp
import numpy as np
import ml_dtypes
from jax import lax
from jax.experimental import pallas as pl
from jax.experimental.pallas import tpu as pltpu
from jax.sharding import PartitionSpec as P

G = 256
DOMX, DOMY = 8, 16
SPANX, SPANY = 32, 16
PADY = 19
MAIN = PADY * SPANX
RIM = 24
N = DOMX * DOMY
ATOM_DEV = 1024
LANES = 768
HALFTILE = 640
CELLS = 704
TILES = LANES // 128
SELFS, PAIRS = 4, 62
REPS = 72
HALF = G
ewald_beta = 0.6
field_scale = 1.0
MESH = pl.DeviceIdType.MESH
f32, bf16 = jnp.float32, jnp.bfloat16


def side_by_side(table):
    high, low = halves(table)
    return np.concatenate([high, low, high], axis=1)


def halves(table):
    high = table.astype(ml_dtypes.bfloat16)
    low = (table - high.astype(np.float64)).astype(ml_dtypes.bfloat16)
    return high, low


def lane_cells():
    lane = np.arange(LANES)
    lane = np.where(lane < CELLS, lane, lane - (CELLS - HALFTILE))
    rim = np.maximum(lane - MAIN, 0)
    x = np.where(lane < MAIN, lane % SPANX, SPANX + rim // RIM)
    y = np.where(lane < MAIN, lane // SPANX, rim % RIM)
    return x, y, (x < SPANX + 3) & (y < PADY)


def self_and_pairs(first, second):
    selfs, pairs, seen = [], [], set()
    for a in range(first):
        for b in range(second):
            if (a, b) in seen:
                continue
            mirror = ((-a) % first, (-b) % second)
            seen.update([(a, b), mirror])
            (selfs if mirror == (a, b) else pairs).append((a, b))
    return selfs, pairs


def modulus(k):
    return 9.0 / (2.0 + np.cos(2.0 * np.pi * k / G)) ** 2


def signed(k):
    return np.where(k < G // 2, k, k - G).astype(np.float64)


def tables():
    out = {}
    wave = np.arange(G // 2)
    grid = np.arange(G)
    turn = 2.0 * np.pi / G
    first = np.cos(turn * (wave[:, None] * grid[None, :] % G))
    second = np.sin(turn * (wave[:, None] * grid[None, :] % G))
    second[0] = np.cos(np.pi * grid)
    out["basis"] = np.concatenate([first, second])

    x, y, valid = lane_cells()
    selfs, pairs = self_and_pairs(DOMX, DOMY)
    reps = selfs + pairs
    weight = np.array([1.0] * SELFS + [2.0] * PAIRS)
    kap = np.array([a for a, b in reps])
    lam = np.array([b for a, b in reps])
    source = np.arange(N)
    c, e = source // DOMY, source % DOMY
    steps = (2 * kap[:, None] * c[None, :] + lam[:, None] * e[None, :]) % 16
    angle = 2.0 * np.pi / 16 * steps
    left = np.zeros((2, REPS, N))
    left[0, : len(reps)] = np.cos(angle)
    left[1, : len(reps)] = np.where(steps % 8 == 0, 0.0, -np.sin(angle))
    kept = np.r_[0 : len(reps), REPS + SELFS : REPS + len(reps)]
    left = left.reshape(2 * REPS, N)
    out["left"], out["left_back"] = left, left[kept].T

    phase = turn * ((kap[:, None] * x[None, :] + lam[:, None] * y[None, :]) % G)
    lane = np.arange(LANES)
    twiddle = np.zeros((2, 2, REPS, LANES))
    for j, kept in enumerate((lane < CELLS, (lane < HALFTILE) | (lane >= CELLS))):
        twiddle[j, 0, : len(reps)] = np.cos(phase) * (valid & kept)
        twiddle[j, 1, : len(reps)] = np.sin(phase) * (valid & kept)
    out["twiddle"] = twiddle

    selfs_in, pairs_in = self_and_pairs(SPANX, SPANY)
    plus = pairs_in + selfs_in[:2]
    minus = [((-a) % SPANX, (-b) % SPANY) for a, b in pairs_in] + selfs_in[2:]

    def inner(modes):
        m = np.array([a for a, b in modes])
        n = np.array([b for a, b in modes])
        return 2.0 * np.pi / 32 * ((x[:, None] * m[None, :] + 2 * y[:, None] * n[None, :]) % 32)

    right = np.concatenate(
        [
            np.cos(inner(plus)),
            np.sin(inner(pairs_in)),
            np.cos(inner(selfs_in[2:])),
        ],
        axis=1,
    )
    out["right"] = right * valid[:, None]
    out["right_back"] = out["right"].T

    rate = (np.pi / (ewald_beta * G)) ** 2
    bump = np.zeros((4, REPS, HALF))
    bump[2:] = 1.0
    for row, modes in enumerate((plus, minus)):
        kx = kap[:, None] + DOMX * np.array([a for a, b in modes])[None, :]
        ky = lam[:, None] + DOMY * np.array([b for a, b in modes])[None, :]
        square = signed(kx) ** 2 + signed(ky) ** 2
        bump[row, : len(reps)] = weight[:, None] * modulus(kx) * modulus(ky) * np.exp(-rate * square)
        bump[2 + row, : len(reps)] = square
    out["bump"] = bump

    strength = field_scale * G**3.5 / math.sqrt(N * ATOM_DEV)
    along = np.zeros((N, 128))
    for j in range(2):
        k = wave.copy()
        share = np.full(N, 2.0)
        share[0] = 1.0
        if j == 1:
            k[0] = G // 2
        square = signed(k) ** 2
        along[:, j] = strength * modulus(k) * np.exp(-rate * square) * share / float(G) ** 3
        along[:, 2 + j] = square
    out["along"] = along
    return out


def far_first():
    hops = (0, 1, 2, 1)
    links = {0: (0, 0), 1: (2, 0), 2: (1, 1), 3: (0, 2)}
    left = [(y, x, c, z) for y in range(4) for x in range(4) for c in range(2) for z in range(4)]
    left = [o for o in left if any(o)]
    used, order = np.zeros(6), []
    while left:
        far = max(hops[o[0]] + hops[o[1]] + hops[o[3]] for o in left)
        best = None
        for o in left:
            if hops[o[0]] + hops[o[1]] + hops[o[3]] < far:
                continue
            load = used + np.array(links[o[0]] + links[o[1]] + links[o[3]])
            key = (load.max(), (load**2).sum())
            if best is None or key < best[0]:
                best = (key, o, load)
        order.append(best[1])
        left.remove(best[1])
        used = best[2]
    return order


def split(value):
    high = value.astype(bf16)
    return high, (value - high.astype(f32)).astype(bf16)


def dot3(a, b, across=0):
    left = jnp.concatenate([a[0], a[1], a[0]], axis=1)
    right = jnp.concatenate([b[0], b[0], b[1]], axis=across)
    return lax.dot_general(left, right, (((1,), (across,)), ((), ())), preferred_element_type=f32)


def dot(a, b):
    return jnp.dot(a, b, preferred_element_type=f32)


def splines(u):
    rest = 1.0 - u
    square = u * u
    cube = square * u
    values = [
        rest * rest * rest / 6.0,
        (3.0 * cube - 6.0 * square + 4.0) / 6.0,
        (-3.0 * cube + 3.0 * square + 3.0 * u + 1.0) / 6.0,
        cube / 6.0,
    ]
    slopes = [
        -0.5 * rest * rest,
        0.5 * (3.0 * square - 4.0 * u),
        0.5 * (-3.0 * square + 2.0 * u + 1.0),
        0.5 * square,
    ]
    return values, slopes


def spread(rows, first, terms, wrap=None):
    shape = (rows, first.shape[1])
    offset = lax.broadcasted_iota(jnp.int32, shape, 0) - first
    if wrap:
        offset = offset & (wrap - 1)
    masks = [offset == a for a in range(4)]
    outs = []
    for term in terms:
        total = jnp.where(masks[3], term[3], 0.0)
        for a in (2, 1, 0):
            total = jnp.where(masks[a], term[a], total)
        outs.append(total)
    return outs


def body(
    charges_any, fractions_any, bases_any, counts, basis_any, left_any, back_any, right_any, wide_any, twiddle_any,
    bump_any, along_any, out, basis, left, left_back, right, right_back, twiddle, bump, along,
    charges, fractions, bases, tw, bt, send_a, send_b, recv_a, recv_b,
    back_a, back_b, home_a, home_b, gt, early, sems, loads,
):
    dom, z = lax.axis_index("dom"), lax.axis_index("grid")
    p = dom * 4 + z
    barrier = pltpu.get_barrier_semaphore()
    loading = [
        pltpu.make_async_copy(source, target, loads.at[k])
        for k, (source, target) in enumerate(
            (
                (fractions_any, fractions), (bases_any, bases), (charges_any, charges), (basis_any, basis),
                (left_any, left), (right_any, right), (twiddle_any, twiddle), (wide_any, right_back),
                (bump_any, bump), (along_any, along), (back_any, left_back),
            )
        )
    ]
    for load in loading:
        load.start()

    ys = [lax.rem(dom // 8 + k, 4) * 8 for k in range(4)]
    xs = [lax.rem(lax.rem(dom, 8) // 2 + k, 4) * 2 for k in range(4)]
    cores = [lax.rem(dom + k, 2) for k in range(2)]
    zs = [lax.rem(z + k, 4) for k in range(4)]
    chips = [[a + b for b in xs] for a in ys]
    peers = [(chips[a][b] + cores[c], zs[k]) for a, b, c, k in far_first()]

    for where in peers:
        pl.semaphore_signal(barrier, inc=1, device_id=where, device_id_type=MESH)

    def post(source, target, which):
        for where in peers:
            pltpu.make_async_remote_copy(
                src_ref=source.at[pl.ds(where[0] * 4 + where[1], 1)], dst_ref=target.at[pl.ds(p, 1)],
                send_sem=sems.at[2 * which], recv_sem=sems.at[2 * which + 1],
                device_id=where, device_id_type=MESH,
            ).start()
        pltpu.make_async_copy(
            source.at[pl.ds(p, 1)], target.at[pl.ds(p, 1)], sems.at[2 * which + 1]
        ).start()

    def arrived(target, which):
        pltpu.make_async_copy(target, target, sems.at[2 * which + 1]).wait()

    def sent(source, which):
        for first, rows in [(0, N - 8)] + [(k, 1) for k in range(N - 8, N - 1)]:
            part = source.at[pl.ds(first, rows)]
            pltpu.make_async_copy(part, part, sems.at[2 * which]).wait()

    for load in loading[:3]:
        load.wait()
    values, slopes = splines(fractions[...])
    alive = lax.broadcasted_iota(jnp.int32, (1, ATOM_DEV), 1) < counts[0]
    weighted = jnp.where(alive, charges[...], 0.0)

    def row(which, terms):
        return [t[which : which + 1] for t in terms]

    (wz,) = spread(G, bases[2:3], (row(2, values),), G)
    wz = split(wz)
    loading[3].wait()
    high, low = split(dot3((basis[0], basis[1]), wz))
    tw[0, 0] = high
    tw[1, 0] = low

    local_x = bases[0:1] - (p // DOMY) * SPANX
    local_y = bases[1:2] - lax.rem(p, DOMY) * SPANY
    wx, sx = spread(40, local_x, (row(0, values), row(0, slopes)))
    wy, sy = spread(RIM, local_y, (row(1, values), row(1, slopes)))
    charged = wx * weighted
    for y in range(PADY):
        high, low = split(charged[:SPANX] * wy[y : y + 1])
        bt[0, pl.ds(y * SPANX, SPANX)] = high
        bt[1, pl.ds(y * SPANX, SPANX)] = low
    rim = [charged[SPANX + a : SPANX + a + 1] * wy for a in range(3)]
    high, low = split(jnp.concatenate(rim + [jnp.zeros((CELLS - MAIN - 3 * RIM, ATOM_DEV), f32)], axis=0))
    for k, part in enumerate((high, low)):
        bt[k, pl.ds(MAIN, CELLS - MAIN)] = part

    planes = dot3((tw[0, 0], tw[1, 0]), (bt[0], bt[1]), 1)

    send_a[:, :HALFTILE] = planes[:N, :HALFTILE]
    send_b[...] = planes[N:, :HALFTILE]
    send_a[:, HALFTILE:] = jnp.concatenate([planes[:N, HALFTILE:], planes[N:, HALFTILE:]], axis=1)
    pl.semaphore_wait(barrier, N - 1)
    post(send_a, recv_a, 0)

    (sz,) = spread(G, bases[2:3], (row(2, slopes),), G)
    high, low = split(dot3((basis[0], basis[1]), split(sz)))
    tw[0, 1] = high
    tw[1, 1] = low
    post(send_b, recv_b, 1)
    for load in loading[4:]:
        load.wait()
    mine = along[pl.ds(p, 1), :]
    lane = lax.broadcasted_iota(jnp.int32, (REPS, HALF), 1)
    paired = lane < HALF - 2
    factors = []
    for j in range(2):
        scale, square = mine[:, j : j + 1], mine[:, 2 + j : 3 + j]
        both = []
        for end in range(2):
            whole = bump[2 + end] + square
            positive = whole > 0.0
            both.append(
                jnp.where(positive, bump[end] * scale / jnp.where(positive, whole, 1.0), 0.0)
            )
        total = both[0] + both[1]
        factors.append(
            (
                jnp.where(paired, total, both[0]),
                jnp.where(paired, total, both[1]),
                jnp.where(paired, both[0] - both[1], 0.0),
            )
        )

    def filtered(arrival, j):
        high, low = split(arrival)
        first = dot(left[...], jnp.concatenate([high, high, low], axis=0))
        real, imag = first[:REPS], first[REPS:]
        tc, ts = twiddle[j, 0], twiddle[j, 1]
        turned = jnp.concatenate([real * tc + imag * ts, imag * tc - real * ts], axis=0)
        wide = (right[0], right[1])
        modes = dot3(split(turned), wide)
        f1, f2, fd = factors[j]
        rc, rs = modes[:REPS, :HALF], modes[:REPS, HALF:]
        ic, is_ = modes[REPS:, :HALF], modes[REPS:, HALF:]
        modes = jnp.concatenate(
            [
                jnp.concatenate([f1 * rc + fd * is_, f2 * rs - fd * ic], axis=1),
                jnp.concatenate([f1 * ic - fd * rs, fd * rc + f2 * is_], axis=1),
            ],
            axis=0,
        )
        cells = dot3(split(modes), (right_back[0], right_back[1]))
        real, imag = cells[:REPS], cells[REPS:]
        turned = jnp.concatenate(
            [(real * tc - imag * ts)[: SELFS + PAIRS], (imag * tc + real * ts)[SELFS : SELFS + PAIRS]],
            axis=0,
        )
        high, low = split(turned)
        return dot(left_back[...], jnp.concatenate([high, high, low], axis=0))

    arrived(recv_a, 0)
    plane = filtered(recv_a[...], 0)
    back_a[...] = plane[:, :HALFTILE]
    back_b[:, HALFTILE:] = plane[:, HALFTILE:]
    post(back_a, home_a, 2)
    arrived(recv_b, 1)
    plane = filtered(jnp.concatenate([recv_b[...], recv_a[:, HALFTILE:]], axis=1), 1)
    back_b[:, :HALFTILE] = plane[:, :HALFTILE]
    back_b[:, HALFTILE:] += plane[:, HALFTILE:]
    post(back_b, home_b, 3)

    sent(send_a, 0)
    sent(send_b, 1)
    chunk = 256

    def fold(part):
        return sum(part[8 * i : 8 * i + 8] for i in range(1, part.shape[0] // 8)) + part[:8]

    def gather(here, field, slope):
        sums = [jnp.zeros((8, chunk), f32) for _ in range(3)]
        for y in range(PADY):
            cells = slice(y * SPANX, (y + 1) * SPANX)
            inner = fold(field[cells] * wx[:SPANX, here])
            sums[0] += fold(field[cells] * sx[:SPANX, here]) * wy[y : y + 1, here]
            sums[1] += inner * sy[y : y + 1, here]
            sums[2] += fold(slope[cells] * wx[:SPANX, here]) * wy[y : y + 1, here]
        for a in range(3):
            cells = slice(MAIN + a * RIM, min(MAIN + (a + 1) * RIM, field.shape[0]))
            if cells.start >= field.shape[0]:
                continue
            x = slice(SPANX + a, SPANX + a + 1)
            rows = slice(0, cells.stop - cells.start)
            sums[0] += fold(field[cells] * wy[rows, here]) * sx[x, here]
            sums[1] += fold(field[cells] * sy[rows, here]) * wx[x, here]
            sums[2] += fold(slope[cells] * wy[rows, here]) * wx[x, here]
        return sums

    def gather_tail(sums, here, field, slope):
        for row in range(HALFTILE, MAIN + 3 * RIM, 8):
            a, y = (row - MAIN) // RIM, (row - MAIN) % RIM
            x, rows = slice(SPANX + a, SPANX + a + 1), slice(y, y + 8)
            cells = slice(row - HALFTILE, row - HALFTILE + 8)
            sums[0] += field[cells] * wy[rows, here] * sx[x, here]
            sums[1] += field[cells] * sy[rows, here] * wx[x, here]
            sums[2] += slope[cells] * wy[rows, here] * wx[x, here]

    def fields(j, part, here):
        rows = slice(j * N, (j + 1) * N)
        high = tw[0, part, rows, here]
        parts = [high, high, tw[1, part, rows, here]]
        if j == 0:
            return dot(gt[0, :HALFTILE, : 3 * N], jnp.concatenate(parts, axis=0))
        other = tw[0, part, :N, here]
        whole = dot(gt[1], jnp.concatenate(parts + [other], axis=0))
        rest = dot(gt[0, HALFTILE:, : 2 * N], jnp.concatenate([other, tw[1, part, :N, here]], axis=0))
        return whole[:HALFTILE], whole[HALFTILE:] + rest

    def turn(home, j):
        for t in range(TILES - 1):
            rows = pl.ds(t * 128, 128)
            high, low = split(home[:, t * 128 : (t + 1) * 128].T)
            gt[j, rows] = jnp.concatenate([high, low, high, jnp.zeros_like(high)], axis=1)

    chunks = [slice(r, r + chunk) for r in range(0, ATOM_DEV, chunk)]
    arrived(home_a, 2)
    turn(home_a, 0)
    for here in chunks:
        for a, part in enumerate(gather(here, fields(0, 0, here), fields(0, 1, here))):
            early[a, :, here] = part
    arrived(home_b, 3)
    turn(home_b, 1)
    shared = home_b[:, HALFTILE:].T
    (high, other), (low, least) = ((part[64:], part[:64]) for part in split(shared))
    gt[1, HALFTILE:] = jnp.concatenate([high, low, high, other], axis=1)
    gt[0, HALFTILE:, : 2 * N] = jnp.concatenate([least, other], axis=1)
    for here in chunks:
        (field, field_tail), (slope, slope_tail) = fields(1, 0, here), fields(1, 1, here)
        sums = gather(here, field, slope)
        gather_tail(sums, here, field_tail, slope_tail)
        for a in range(3):
            total = jnp.sum(sums[a] + early[a, :, here], axis=0, keepdims=True)
            out[a : a + 1, here] = -weighted[:, here] * total
    sent(back_a, 2)
    sent(back_b, 3)


def solution(mesh):
    table = tables()
    pairs = {k: np.stack(halves(table[k])) for k in ("basis", "right", "right_back")}
    pairs.update({k: side_by_side(table[k]) for k in ("left", "left_back")})
    plain = {k: table[k].astype(np.float32) for k in ("twiddle", "bump", "along")}
    held = [pairs[k] for k in ("basis", "left", "left_back", "right", "right_back")]
    held += [plain["twiddle"], plain["bump"], plain["along"]]
    vmem = pl.BlockSpec(memory_space=pltpu.VMEM)
    smem = pl.BlockSpec(memory_space=pltpu.SMEM)
    anywhere = pl.BlockSpec(memory_space=pl.ANY)
    five, six = (pltpu.VMEM((N, lanes), f32) for lanes in (HALFTILE, LANES))
    call = pl.pallas_call(
        body,
        out_shape=pltpu.VMEM((3, ATOM_DEV), f32),
        in_specs=[anywhere] * 3 + [smem] + [anywhere] * 8,
        out_specs=vmem,
        scratch_shapes=[pltpu.VMEM(a.shape, bf16 if a.dtype != np.float32 else f32) for a in held]
        + [
            pltpu.VMEM((1, ATOM_DEV), f32),
            pltpu.VMEM((3, ATOM_DEV), f32),
            pltpu.VMEM((3, ATOM_DEV), jnp.int32),
            pltpu.VMEM((2, 2, G, ATOM_DEV), bf16),
            pltpu.VMEM((2, CELLS, ATOM_DEV), bf16),
            six, five, six, five,
            five, six, five, six,
            pltpu.VMEM((2, CELLS, 4 * N), bf16),
            pltpu.VMEM((3, 8, ATOM_DEV), f32),
            pltpu.SemaphoreType.DMA((8,)),
            pltpu.SemaphoreType.DMA((11,)),
        ],
        compiler_params=pltpu.CompilerParams(
            collective_id=1, has_side_effects=True, vmem_limit_bytes=56 << 20
        ),
    )

    def local(charges, fractions, bases, counts):
        return call(
            charges.reshape(1, ATOM_DEV), fractions, bases, counts, *held
        )

    placed = (
        P(("dom", "grid")),
        P(None, ("dom", "grid")),
        P(None, ("dom", "grid")),
        P(("dom", "grid")),
    )
    return jax.shard_map(
        local, mesh=mesh, in_specs=placed, out_specs=P(None, ("dom", "grid")), check_vma=False
    )
```

```python
import functools
import math

import jax
import jax.numpy as jnp
import numpy as np
import ml_dtypes
from jax import lax
from jax.experimental import pallas as pl
from jax.experimental.pallas import tpu as pltpu
from jax.sharding import PartitionSpec as P

G = 256
DOMX, DOMY = 8, 16
SPANX, SPANY = 32, 16
PADY = 19
MAIN = PADY * SPANX
RIM = 24
N = DOMX * DOMY
ATOM_DEV = 1024
LANES = 768
HALFTILE = 640
CELLS = 704
TILES = LANES // 128
SELFS, PAIRS = 4, 62
REPS = 72
HALF = G
ewald_beta = 0.6
field_scale = 1.0
MESH = pl.DeviceIdType.MESH
f32, bf16 = jnp.float32, jnp.bfloat16


def side_by_side(table):
    high, low = halves(table)
    return np.concatenate([high, low, high], axis=1)


def halves(table):
    high = table.astype(ml_dtypes.bfloat16)
    low = (table - high.astype(np.float64)).astype(ml_dtypes.bfloat16)
    return high, low


def lane_cells():
    lane = np.arange(LANES)
    lane = np.where(lane < CELLS, lane, lane - (CELLS - HALFTILE))
    rim = np.maximum(lane - MAIN, 0)
    x = np.where(lane < MAIN, lane % SPANX, SPANX + rim // RIM)
    y = np.where(lane < MAIN, lane // SPANX, rim % RIM)
    return x, y, (x < SPANX + 3) & (y < PADY)


def self_and_pairs(first, second):
    selfs, pairs, seen = [], [], set()
    for a in range(first):
        for b in range(second):
            if (a, b) in seen:
                continue
            mirror = ((-a) % first, (-b) % second)
            seen.update([(a, b), mirror])
            (selfs if mirror == (a, b) else pairs).append((a, b))
    return selfs, pairs


def modulus(k):
    return 9.0 / (2.0 + np.cos(2.0 * np.pi * k / G)) ** 2


def signed(k):
    return np.where(k < G // 2, k, k - G).astype(np.float64)


def tables():
    out = {}
    wave = np.arange(G // 2)
    grid = np.arange(G)
    turn = 2.0 * np.pi / G
    first = np.cos(turn * (wave[:, None] * grid[None, :] % G))
    second = np.sin(turn * (wave[:, None] * grid[None, :] % G))
    second[0] = np.cos(np.pi * grid)
    out["basis"] = np.concatenate([first, second])

    x, y, valid = lane_cells()
    selfs, pairs = self_and_pairs(DOMX, DOMY)
    reps = selfs + pairs
    weight = np.array([1.0] * SELFS + [2.0] * PAIRS)
    kap = np.array([a for a, b in reps])
    lam = np.array([b for a, b in reps])
    source = np.arange(N)
    c, e = source // DOMY, source % DOMY
    steps = (2 * kap[:, None] * c[None, :] + lam[:, None] * e[None, :]) % 16
    angle = 2.0 * np.pi / 16 * steps
    left = np.zeros((2, REPS, N))
    left[0, : len(reps)] = np.cos(angle)
    left[1, : len(reps)] = np.where(steps % 8 == 0, 0.0, -np.sin(angle))
    kept = np.r_[0 : len(reps), REPS + SELFS : REPS + len(reps)]
    left = left.reshape(2 * REPS, N)
    out["left"], out["left_back"] = left, left[kept].T

    phase = turn * ((kap[:, None] * x[None, :] + lam[:, None] * y[None, :]) % G)
    lane = np.arange(LANES)
    twiddle = np.zeros((2, 2, REPS, LANES))
    for j, kept in enumerate((lane < CELLS, (lane < HALFTILE) | (lane >= CELLS))):
        twiddle[j, 0, : len(reps)] = np.cos(phase) * (valid & kept)
        twiddle[j, 1, : len(reps)] = np.sin(phase) * (valid & kept)
    out["twiddle"] = twiddle

    selfs_in, pairs_in = self_and_pairs(SPANX, SPANY)
    plus = pairs_in + selfs_in[:2]
    minus = [((-a) % SPANX, (-b) % SPANY) for a, b in pairs_in] + selfs_in[2:]

    def inner(modes):
        m = np.array([a for a, b in modes])
        n = np.array([b for a, b in modes])
        return 2.0 * np.pi / 32 * ((x[:, None] * m[None, :] + 2 * y[:, None] * n[None, :]) % 32)

    right = np.concatenate(
        [
            np.cos(inner(plus)),
            np.sin(inner(pairs_in)),
            np.cos(inner(selfs_in[2:])),
        ],
        axis=1,
    )
    out["right"] = right * valid[:, None]
    out["right_back"] = out["right"].T

    rate = (np.pi / (ewald_beta * G)) ** 2
    bump = np.zeros((4, REPS, HALF))
    bump[2:] = 1.0
    for row, modes in enumerate((plus, minus)):
        kx = kap[:, None] + DOMX * np.array([a for a, b in modes])[None, :]
        ky = lam[:, None] + DOMY * np.array([b for a, b in modes])[None, :]
        square = signed(kx) ** 2 + signed(ky) ** 2
        bump[row, : len(reps)] = weight[:, None] * modulus(kx) * modulus(ky) * np.exp(-rate * square)
        bump[2 + row, : len(reps)] = square
    out["bump"] = bump

    strength = field_scale * G**3.5 / math.sqrt(N * ATOM_DEV)
    along = np.zeros((N, 128))
    for j in range(2):
        k = wave.copy()
        share = np.full(N, 2.0)
        share[0] = 1.0
        if j == 1:
            k[0] = G // 2
        square = signed(k) ** 2
        along[:, j] = strength * modulus(k) * np.exp(-rate * square) * share / float(G) ** 3
        along[:, 2 + j] = square
    out["along"] = along
    return out


def far_first():
    hops = (0, 1, 2, 1)
    links = {0: (0, 0), 1: (2, 0), 2: (1, 1), 3: (0, 2)}
    left = [(y, x, c, z) for y in range(4) for x in range(4) for c in range(2) for z in range(4)]
    left = [o for o in left if any(o)]
    used, order = np.zeros(6), []
    while left:
        far = max(hops[o[0]] + hops[o[1]] + hops[o[3]] for o in left)
        best = None
        for o in left:
            if hops[o[0]] + hops[o[1]] + hops[o[3]] < far:
                continue
            load = used + np.array(links[o[0]] + links[o[1]] + links[o[3]])
            key = (load.max(), (load**2).sum())
            if best is None or key < best[0]:
                best = (key, o, load)
        order.append(best[1])
        left.remove(best[1])
        used = best[2]
    return order


def split(value):
    high = value.astype(bf16)
    return high, (value - high.astype(f32)).astype(bf16)


def dot3(a, b, across=0):
    left = jnp.concatenate([a[0], a[1], a[0]], axis=1)
    right = jnp.concatenate([b[0], b[0], b[1]], axis=across)
    return lax.dot_general(left, right, (((1,), (across,)), ((), ())), preferred_element_type=f32)


def dot(a, b):
    return jnp.dot(a, b, preferred_element_type=f32)


def splines(u):
    rest = 1.0 - u
    square = u * u
    cube = square * u
    values = [
        rest * rest * rest / 6.0,
        (3.0 * cube - 6.0 * square + 4.0) / 6.0,
        (-3.0 * cube + 3.0 * square + 3.0 * u + 1.0) / 6.0,
        cube / 6.0,
    ]
    slopes = [
        -0.5 * rest * rest,
        0.5 * (3.0 * square - 4.0 * u),
        0.5 * (-3.0 * square + 2.0 * u + 1.0),
        0.5 * square,
    ]
    return values, slopes


def spread(rows, first, terms, wrap=None):
    shape = (rows, first.shape[1])
    offset = lax.broadcasted_iota(jnp.int32, shape, 0) - first
    if wrap:
        offset = offset & (wrap - 1)
    masks = [offset == a for a in range(4)]
    outs = []
    for term in terms:
        total = jnp.where(masks[3], term[3], 0.0)
        for a in (2, 1, 0):
            total = jnp.where(masks[a], term[a], total)
        outs.append(total)
    return outs


def body(
    charges_any, fractions_any, bases_any, counts, basis_any, left_any, back_any, right_any, wide_any, twiddle_any,
    bump_any, along_any, out, basis, left, left_back, right, right_back, twiddle, bump, along,
    charges, fractions, bases, tw, bt, send_a, send_b, recv_a, recv_b,
    back_a, back_b, home_a, home_b, gt, early, sems, loads,
):
    dom, z = lax.axis_index("dom"), lax.axis_index("grid")
    p = dom * 4 + z
    barrier = pltpu.get_barrier_semaphore()
    loading = [
        pltpu.make_async_copy(source, target, loads.at[k])
        for k, (source, target) in enumerate(
            (
                (fractions_any, fractions), (bases_any, bases), (charges_any, charges), (basis_any, basis),
                (left_any, left), (right_any, right), (twiddle_any, twiddle), (wide_any, right_back),
                (bump_any, bump), (along_any, along), (back_any, left_back),
            )
        )
    ]
    for load in loading:
        load.start()

    ys = [lax.rem(dom // 8 + k, 4) * 8 for k in range(4)]
    xs = [lax.rem(lax.rem(dom, 8) // 2 + k, 4) * 2 for k in range(4)]
    cores = [lax.rem(dom + k, 2) for k in range(2)]
    zs = [lax.rem(z + k, 4) for k in range(4)]
    chips = [[a + b for b in xs] for a in ys]
    peers = [(chips[a][b] + cores[c], zs[k]) for a, b, c, k in far_first()]

    for where in peers:
        pl.semaphore_signal(barrier, inc=1, device_id=where, device_id_type=MESH)

    def post(source, target, which):
        for where in peers:
            pltpu.make_async_remote_copy(
                src_ref=source.at[pl.ds(where[0] * 4 + where[1], 1)], dst_ref=target.at[pl.ds(p, 1)],
                send_sem=sems.at[2 * which], recv_sem=sems.at[2 * which + 1],
                device_id=where, device_id_type=MESH,
            ).start()
        pltpu.make_async_copy(
            source.at[pl.ds(p, 1)], target.at[pl.ds(p, 1)], sems.at[2 * which + 1]
        ).start()

    def arrived(target, which):
        pltpu.make_async_copy(target, target, sems.at[2 * which + 1]).wait()

    def sent(source, which):
        for first, rows in [(0, N - 8)] + [(k, 1) for k in range(N - 8, N - 1)]:
            part = source.at[pl.ds(first, rows)]
            pltpu.make_async_copy(part, part, sems.at[2 * which]).wait()

    for load in loading[:3]:
        load.wait()
    values, slopes = splines(fractions[...])
    alive = lax.broadcasted_iota(jnp.int32, (1, ATOM_DEV), 1) < counts[0]
    weighted = jnp.where(alive, charges[...], 0.0)

    def row(which, terms):
        return [t[which : which + 1] for t in terms]

    (wz,) = spread(G, bases[2:3], (row(2, values),), G)
    wz = split(wz)
    loading[3].wait()
    high, low = split(dot3((basis[0], basis[1]), wz))
    tw[0, 0] = high
    tw[1, 0] = low

    local_x = bases[0:1] - (p // DOMY) * SPANX
    local_y = bases[1:2] - lax.rem(p, DOMY) * SPANY
    wx, sx = spread(40, local_x, (row(0, values), row(0, slopes)))
    wy, sy = spread(RIM, local_y, (row(1, values), row(1, slopes)))
    charged = wx * weighted
    for y in range(PADY):
        high, low = split(charged[:SPANX] * wy[y : y + 1])
        bt[0, pl.ds(y * SPANX, SPANX)] = high
        bt[1, pl.ds(y * SPANX, SPANX)] = low
    rim = [charged[SPANX + a : SPANX + a + 1] * wy for a in range(3)]
    high, low = split(jnp.concatenate(rim + [jnp.zeros((CELLS - MAIN - 3 * RIM, ATOM_DEV), f32)], axis=0))
    for k, part in enumerate((high, low)):
        bt[k, pl.ds(MAIN, CELLS - MAIN)] = part

    def planes(rows, first, last):
        cells = slice(first, last)
        return dot3((tw[0, 0, rows], tw[1, 0, rows]), (bt[0, cells], bt[1, cells]), 1)

    plane = planes(slice(0, N), 0, CELLS)
    send_a[:, :HALFTILE] = plane[:, :HALFTILE]
    send_a[:, HALFTILE:] = jnp.concatenate(
        [plane[:, HALFTILE:], planes(slice(N, G), HALFTILE, CELLS)], axis=1
    )
    pl.semaphore_wait(barrier, N - 1)
    post(send_a, recv_a, 0)

    send_b[...] = planes(slice(N, G), 0, HALFTILE)
    post(send_b, recv_b, 1)

    (sz,) = spread(G, bases[2:3], (row(2, slopes),), G)
    high, low = split(dot3((basis[0], basis[1]), split(sz)))
    tw[0, 1] = high
    tw[1, 1] = low
    for load in loading[4:]:
        load.wait()
    mine = along[pl.ds(p, 1), :]
    lane = lax.broadcasted_iota(jnp.int32, (REPS, HALF), 1)
    paired = lane < HALF - 2
    factors = []
    for j in range(2):
        scale, square = mine[:, j : j + 1], mine[:, 2 + j : 3 + j]
        both = []
        for end in range(2):
            whole = bump[2 + end] + square
            positive = whole > 0.0
            both.append(
                jnp.where(positive, bump[end] * scale / jnp.where(positive, whole, 1.0), 0.0)
            )
        total = both[0] + both[1]
        factors.append(
            (
                jnp.where(paired, total, both[0]),
                jnp.where(paired, total, both[1]),
                jnp.where(paired, both[0] - both[1], 0.0),
            )
        )

    def filtered(arrival, j):
        high, low = split(arrival)
        first = dot(left[...], jnp.concatenate([high, high, low], axis=0))
        real, imag = first[:REPS], first[REPS:]
        tc, ts = twiddle[j, 0], twiddle[j, 1]
        turned = jnp.concatenate([real * tc + imag * ts, imag * tc - real * ts], axis=0)
        wide = (right[0], right[1])
        modes = dot3(split(turned), wide)
        f1, f2, fd = factors[j]
        rc, rs = modes[:REPS, :HALF], modes[:REPS, HALF:]
        ic, is_ = modes[REPS:, :HALF], modes[REPS:, HALF:]
        modes = jnp.concatenate(
            [
                jnp.concatenate([f1 * rc + fd * is_, f2 * rs - fd * ic], axis=1),
                jnp.concatenate([f1 * ic - fd * rs, fd * rc + f2 * is_], axis=1),
            ],
            axis=0,
        )
        cells = dot3(split(modes), (right_back[0], right_back[1]))
        real, imag = cells[:REPS], cells[REPS:]
        turned = jnp.concatenate(
            [(real * tc - imag * ts)[: SELFS + PAIRS], (imag * tc + real * ts)[SELFS : SELFS + PAIRS]],
            axis=0,
        )
        high, low = split(turned)
        return dot(left_back[...], jnp.concatenate([high, high, low], axis=0))

    arrived(recv_a, 0)
    plane = filtered(recv_a[...], 0)
    back_a[...] = plane[:, :HALFTILE]
    back_b[:, HALFTILE:] = plane[:, HALFTILE:]
    post(back_a, home_a, 2)
    arrived(recv_b, 1)
    plane = filtered(jnp.concatenate([recv_b[...], recv_a[:, HALFTILE:]], axis=1), 1)
    back_b[:, :HALFTILE] = plane[:, :HALFTILE]
    back_b[:, HALFTILE:] += plane[:, HALFTILE:]
    post(back_b, home_b, 3)

    sent(send_a, 0)
    sent(send_b, 1)
    chunk = 256

    def fold(part):
        return sum(part[8 * i : 8 * i + 8] for i in range(1, part.shape[0] // 8)) + part[:8]

    def gather(here, field, slope):
        sums = [jnp.zeros((8, chunk), f32) for _ in range(3)]
        for y in range(PADY):
            cells = slice(y * SPANX, (y + 1) * SPANX)
            inner = fold(field[cells] * wx[:SPANX, here])
            sums[0] += fold(field[cells] * sx[:SPANX, here]) * wy[y : y + 1, here]
            sums[1] += inner * sy[y : y + 1, here]
            sums[2] += fold(slope[cells] * wx[:SPANX, here]) * wy[y : y + 1, here]
        for a in range(3):
            cells = slice(MAIN + a * RIM, min(MAIN + (a + 1) * RIM, field.shape[0]))
            if cells.start >= field.shape[0]:
                continue
            x = slice(SPANX + a, SPANX + a + 1)
            rows = slice(0, cells.stop - cells.start)
            sums[0] += fold(field[cells] * wy[rows, here]) * sx[x, here]
            sums[1] += fold(field[cells] * sy[rows, here]) * wx[x, here]
            sums[2] += fold(slope[cells] * wy[rows, here]) * wx[x, here]
        return sums

    def gather_tail(sums, here, field, slope):
        for row in range(HALFTILE, MAIN + 3 * RIM, 8):
            a, y = (row - MAIN) // RIM, (row - MAIN) % RIM
            x, rows = slice(SPANX + a, SPANX + a + 1), slice(y, y + 8)
            cells = slice(row - HALFTILE, row - HALFTILE + 8)
            sums[0] += field[cells] * wy[rows, here] * sx[x, here]
            sums[1] += field[cells] * sy[rows, here] * wx[x, here]
            sums[2] += slope[cells] * wy[rows, here] * wx[x, here]

    def fields(j, part, here):
        rows = slice(j * N, (j + 1) * N)
        high = tw[0, part, rows, here]
        parts = [high, high, tw[1, part, rows, here]]
        if j == 0:
            return dot(gt[0, :HALFTILE, : 3 * N], jnp.concatenate(parts, axis=0))
        other = tw[0, part, :N, here]
        whole = dot(gt[1], jnp.concatenate(parts + [other], axis=0))
        rest = dot(gt[0, HALFTILE:, : 2 * N], jnp.concatenate([other, tw[1, part, :N, here]], axis=0))
        return whole[:HALFTILE], whole[HALFTILE:] + rest

    def turn(home, j):
        for t in range(TILES - 1):
            rows = pl.ds(t * 128, 128)
            high, low = split(home[:, t * 128 : (t + 1) * 128].T)
            gt[j, rows] = jnp.concatenate([high, low, high, jnp.zeros_like(high)], axis=1)

    chunks = [slice(r, r + chunk) for r in range(0, ATOM_DEV, chunk)]
    arrived(home_a, 2)
    turn(home_a, 0)
    for here in chunks:
        for a, part in enumerate(gather(here, fields(0, 0, here), fields(0, 1, here))):
            early[a, :, here] = part
    arrived(home_b, 3)
    turn(home_b, 1)
    shared = home_b[:, HALFTILE:].T
    (high, other), (low, least) = ((part[64:], part[:64]) for part in split(shared))
    gt[1, HALFTILE:] = jnp.concatenate([high, low, high, other], axis=1)
    gt[0, HALFTILE:, : 2 * N] = jnp.concatenate([least, other], axis=1)
    for here in chunks:
        (field, field_tail), (slope, slope_tail) = fields(1, 0, here), fields(1, 1, here)
        sums = gather(here, field, slope)
        gather_tail(sums, here, field_tail, slope_tail)
        for a in range(3):
            total = jnp.sum(sums[a] + early[a, :, here], axis=0, keepdims=True)
            out[a : a + 1, here] = -weighted[:, here] * total
    sent(back_a, 2)
    sent(back_b, 3)


def solution(mesh):
    table = tables()
    pairs = {k: np.stack(halves(table[k])) for k in ("basis", "right", "right_back")}
    pairs.update({k: side_by_side(table[k]) for k in ("left", "left_back")})
    plain = {k: table[k].astype(np.float32) for k in ("twiddle", "bump", "along")}
    held = [pairs[k] for k in ("basis", "left", "left_back", "right", "right_back")]
    held += [plain["twiddle"], plain["bump"], plain["along"]]
    vmem = pl.BlockSpec(memory_space=pltpu.VMEM)
    smem = pl.BlockSpec(memory_space=pltpu.SMEM)
    anywhere = pl.BlockSpec(memory_space=pl.ANY)
    five, six = (pltpu.VMEM((N, lanes), f32) for lanes in (HALFTILE, LANES))
    call = pl.pallas_call(
        body,
        out_shape=pltpu.VMEM((3, ATOM_DEV), f32),
        in_specs=[anywhere] * 3 + [smem] + [anywhere] * 8,
        out_specs=vmem,
        scratch_shapes=[pltpu.VMEM(a.shape, bf16 if a.dtype != np.float32 else f32) for a in held]
        + [
            pltpu.VMEM((1, ATOM_DEV), f32),
            pltpu.VMEM((3, ATOM_DEV), f32),
            pltpu.VMEM((3, ATOM_DEV), jnp.int32),
            pltpu.VMEM((2, 2, G, ATOM_DEV), bf16),
            pltpu.VMEM((2, CELLS, ATOM_DEV), bf16),
            six, five, six, five,
            five, six, five, six,
            pltpu.VMEM((2, CELLS, 4 * N), bf16),
            pltpu.VMEM((3, 8, ATOM_DEV), f32),
            pltpu.SemaphoreType.DMA((8,)),
            pltpu.SemaphoreType.DMA((11,)),
        ],
        compiler_params=pltpu.CompilerParams(
            collective_id=1, has_side_effects=True, vmem_limit_bytes=56 << 20
        ),
    )

    def local(charges, fractions, bases, counts):
        return call(
            charges.reshape(1, ATOM_DEV), fractions, bases, counts, *held
        )

    placed = (
        P(("dom", "grid")),
        P(None, ("dom", "grid")),
        P(None, ("dom", "grid")),
        P(("dom", "grid")),
    )
    return jax.shard_map(
        local, mesh=mesh, in_specs=placed, out_specs=P(None, ("dom", "grid")), check_vma=False
    )
```
